256 devices in a mesh: shot: 32 (over z_hi, y, x), slab: 8 (over z_lo, core).
Axes of the slice: x: 4, y: 4, z: 8 (z_hi: 2, z_lo: 4; z = z_hi * 4 + z_lo), core: 2. Of those that a mesh axis runs over, the one named last changes fastest.
Arguments:
- waves: float32 [32, 2, 5, 64, 4096], P('shot', None, None, 'slab'), may hold values from -6 to 6
- traces: float32 [32, 16, 1024], P('shot', None, 'slab'), may hold values from -6 to 6
- rec_tile: int32 [32, 1024, 1], P('shot', 'slab'), may hold values from 0 to 7; in each aligned block of 128 rows (0 to 127, 128 to 255, ..., all dimensions but the last counted through in order) at most 48 rows name the same one
- rec_col: int32 [32, 1024], P('shot', 'slab'), may hold values from 0 to 7
- offsets: int32 [32], replicated, may hold values from 0 to 7
- directory: int32 [8], replicated, may hold values from 0 to 7, each once
- model_store: bfloat16 [7, 8, 64, 4096], P(None, None, 'slab', 'shot'), as said below
Outputs:
- waves_out: float32 [32, 2, 5, 64, 4096], P('shot', None, None, 'slab')
- image_stack: float32 [8, 64, 4096], P(None, 'slab', 'shot')
The draws below stay inside these ranges and needn't reach their ends.
Inputs may be any that keep to these rules, and one draw needn't show every extreme that they name: `rec_tile`: within the receivers of one shot held by one slab index (aligned blocks of 128), at most 48 lie in the same slab. directory is a permutation. `model_store`: in every cell the first six entries form a positive-definite stiffness of a tilted transversely isotropic medium and the seventh, the buoyancy, is positive.
All inputs are finite; a program needn't handle non-finite values.
Results may differ from the reference program's by a relative error of at most 0.00045.
Values may be sent and summed in bfloat16 or wider, within the bound.
No kernel may reach another device: no remote copies, remote signals or barrier semaphores. Data moves between devices by JAX's collectives and lax.ppermute only.
A program may use at most 128 MiB of HBM per device.

```python
import math
import jax
import jax.numpy as jnp
import numpy as np
from jax import lax

CX = 8
NZ = 4096
STEPS = 16
PML = 16
REC_DEPTH = 24
REC_DEV = 128
NBLK = 8
SHOTS = 32
NXA = 64
NREC = 1024
CAP = 48
N_SLAB = 8


def draw_model_store(key, part):
    keys = jax.random.split(jax.random.fold_in(key, 17), 6)
    shape = (NBLK, NXA, NZ)
    c33 = jax.random.uniform(keys[0], shape, jnp.float32, 0.08, 0.2)
    c55 = c33 * jax.random.uniform(keys[1], shape, jnp.float32, 0.15, 0.35)
    epsilon = jax.random.uniform(keys[2], shape, jnp.float32, 0.0, 0.25)
    delta = jax.random.uniform(keys[3], shape, jnp.float32, -0.05, 0.15)
    theta = jax.random.uniform(keys[4], shape, jnp.float32, -0.8, 0.8)
    buoyancy = jnp.exp(jax.random.uniform(keys[5], shape, jnp.float32, -0.6931, 0.0))
    c11 = c33 * (1.0 + 2.0 * epsilon)
    c13 = jnp.sqrt((c33 - c55) * (2.0 * delta * c33 + c33 - c55)) - c55
    cosine = jnp.cos(theta)
    sine = jnp.sin(theta)
    cc = cosine * cosine
    ss = sine * sine
    cs = cosine * sine
    shear = c13 + 2.0 * c55
    r11 = c11 * cc * cc + 2.0 * shear * ss * cc + c33 * ss * ss
    r33 = c11 * ss * ss + 2.0 * shear * ss * cc + c33 * cc * cc
    r13 = (c11 + c33 - 4.0 * c55) * ss * cc + c13 * (ss * ss + cc * cc)
    r55 = (c11 + c33 - 2.0 * c13 - 2.0 * c55) * ss * cc + c55 * (cc - ss) * (cc - ss)
    r15 = cs * (c11 * cc - c33 * ss - shear * (cc - ss))
    r35 = cs * (c11 * ss - c33 * cc + shear * (cc - ss))
    stacked = jnp.stack([r11, r13, r15, r33, r35, r55, buoyancy], axis=0)
    return stacked.astype(jnp.bfloat16)


def place_ends(entries, own_key, smallest, largest):
    index_at = [jax.random.randint(jax.random.fold_in(own_key, axis), (), 0, length) for axis, length in enumerate(entries.shape)]
    main_axis = entries.shape.index(max(entries.shape))
    beside = index_at[:main_axis] + [(index_at[main_axis] + 1) % entries.shape[main_axis]] + index_at[main_axis + 1:]
    return entries.at[tuple(index_at)].set(smallest).at[tuple(beside)].set(largest)


def level_of(key, dims, cuts, smallest, top_value):
    loudness = 1.0
    for dim, blocks in cuts:
        steps = jax.random.uniform(jax.random.fold_in(jax.random.fold_in(key, 6), dim), (blocks,), jnp.float32, smallest / len(cuts), top_value / len(cuts))
        loudness = loudness * jnp.repeat(jnp.exp(steps), dims[dim] // blocks).reshape((-1,) + (1,) * (len(dims) - 1 - dim))
    return loudness


def routed_block(key, own, number, rows, amount, top, most, lean):
    order = jax.random.permutation(key, amount)
    packed, ordinary = shares(amount, rows * top, most, lean, True), shares(amount, rows * top, most, lean, False)
    places = jnp.arange(amount)

    def named(lengths, rotation):
        used = int((lengths > 0).sum())
        fixed = max(1, used // 4)
        shifted = fixed + (places - fixed + rotation * (used - fixed)) % max(1, amount - fixed)
        return jnp.zeros((amount,), jnp.int32).at[order[jnp.where(places < fixed, places, shifted)]].set(jnp.asarray(lengths, jnp.int32))

    lengths = jnp.where(number % 4 == 0, named(packed, number // 4), named(ordinary, number - number // 4 - 1))
    mixed = jax.random.permutation(jax.random.fold_in(own, 3), amount)
    source_of, sink = mixed[0:amount // 2 * 2:2], mixed[1:amount // 2 * 2:2]
    slack = jnp.minimum(lengths[source_of] - 1, most - lengths[sink]) // 2
    slack = jnp.where((source_of == order[0]) | (sink == order[0]) | (lengths[sink] == 0), 0, jnp.maximum(slack, 0))
    shifted = jax.random.randint(jax.random.fold_in(own, 4), (amount // 2,), 0, 1 << 20) % (slack + 1)
    lengths = lengths.at[source_of].add(-shifted).at[sink].add(shifted)
    members = jnp.searchsorted(jnp.cumsum(lengths), jnp.arange(rows * top), side="right").astype(jnp.int32)
    listing = members.reshape(top, rows).T
    listing = listing[jax.random.permutation(jax.random.fold_in(own, 1), rows)]
    rotation = jax.random.randint(jax.random.fold_in(own, 2), (rows, 1), 0, top)
    return jnp.take_along_axis(listing, (jnp.arange(top)[None, :] + rotation) % top, axis=1)


def shares(count, total, most, lean, full):
    loads = [(1 << 20) // math.isqrt(rank ** lean) + 1 for rank in range(1, count + 1)]
    largest = most if full else min(most, max(-(-total // count), total * loads[0] // sum(loads)))
    least = 1 if total - largest >= count - 1 else 0
    holding, spare = [largest] + [least] * (count - 1), total - largest - least * (count - 1)
    while spare > 0:
        free = [i for i in range(1, count) if holding[i] < largest] or [i for i in range(1, count) if holding[i] < most]
        mass, left = sum([loads[i] for i in free]), spare
        for i in free:
            addition = min(most - holding[i], max(1, left * loads[i] // mass), spare)
            holding[i] = holding[i] + addition
            spare = spare - addition
    return np.array(holding)


def gaussian(rng, dims, scale, reach, pieces=(), kind=jnp.bfloat16):
    loudness = level_of(rng, dims, pieces, -0.22, 0.18) if pieces else 1.0
    drawn = jax.random.normal(rng, dims, jnp.float32) * scale * loudness
    return jnp.minimum(jnp.maximum(drawn, -reach), reach).astype(kind)


def setup_inputs(seed: int = 0) -> dict:
    seeds = jax.random.split(jax.random.key(seed), 8)
    waves = gaussian(seeds[0], (SHOTS, 2, 5, NXA, NZ), 1.0, 6.0, ((0, 32), (3, 8)), jnp.float32)
    traces = gaussian(seeds[1], (SHOTS, STEPS, NREC), 1.0, 6.0, ((0, 32), (2, 8)), jnp.float32)
    rec_tile_keys = jax.random.split(jax.random.fold_in(seeds[2], 1), SHOTS * NREC // REC_DEV)
    rec_tile_turns = jax.random.permutation(jax.random.fold_in(seeds[2], 3), SHOTS * NREC // REC_DEV)
    rec_tile = jax.vmap(lambda own, number: routed_block(jax.random.fold_in(seeds[2], 2), own, number, REC_DEV, N_SLAB, 1, CAP, 2))(rec_tile_keys, rec_tile_turns).reshape((SHOTS, NREC, 1))
    rec_col = place_ends(jax.random.randint(seeds[3], (SHOTS, NREC), 0, CX), jax.random.fold_in(seeds[3], 1), 0, CX - 1).astype(jnp.int32)
    offsets = place_ends(jax.random.randint(seeds[4], (SHOTS,), 0, NBLK), jax.random.fold_in(seeds[4], 1), 0, NBLK - 1).astype(jnp.int32)
    directory = jax.random.permutation(seeds[5], NBLK).astype(jnp.int32)
    model_store = draw_model_store(jax.random.fold_in(seeds[7], 71), 0)
    return dict(waves=waves, traces=traces, rec_tile=rec_tile, rec_col=rec_col, offsets=offsets, directory=directory, model_store=model_store)


damping_peak = 0.2


def z_below(array):
    return jnp.concatenate([jnp.zeros_like(array[..., :1]), array[..., :-1]], axis=-1)


def z_above(array):
    return jnp.concatenate([array[..., 1:], jnp.zeros_like(array[..., :1])], axis=-1)


def damping(x_index, total_x, depth_count):
    z_index = jnp.arange(depth_count, dtype=jnp.int32)
    wide_x = jnp.maximum(jnp.maximum(PML - x_index, x_index - (total_x - 1 - PML)), 0).astype(jnp.float32) / PML
    wide_z = jnp.maximum(jnp.maximum(PML - z_index, z_index - (depth_count - 1 - PML)), 0).astype(jnp.float32) / PML
    return 1.0 - damping_peak * (wide_x[:, None] * wide_x[:, None] + wide_z[None, :] * wide_z[None, :])


def velocity_update(waves, coefs, signs, stress_left, inject_row):
    stress = waves[:, 2:5]
    extended = jnp.concatenate([stress_left, stress], axis=2)
    here = extended[:, :, 1:]
    left = extended[:, :, :-1]
    here_z = z_below(here)
    left_z = z_below(left)
    grad_x = 0.5 * ((here + here_z) - (left + left_z))
    grad_z = 0.5 * ((here + left) - (here_z + left_z))
    buoyant = signs * coefs[6]
    vel_x = waves[:, 0] + buoyant * (grad_x[:, 0] + grad_z[:, 2])
    vel_z = waves[:, 1] + buoyant * (grad_x[:, 2] + grad_z[:, 1])
    vel_z = vel_z.at[1, :, REC_DEPTH].add(inject_row)
    return jnp.concatenate([jnp.stack([vel_x, vel_z], axis=1), stress], axis=1)


def stress_update(waves, coefs, signs, vel_right, profile):
    velocity = waves[:, 0:2]
    extended = jnp.concatenate([velocity, vel_right], axis=2)
    here = extended[:, :, :-1]
    right = extended[:, :, 1:]
    here_z = z_above(here)
    right_z = z_above(right)
    grad_x = 0.5 * ((right + right_z) - (here + here_z))
    grad_z = 0.5 * ((here_z + right_z) - (here + right))
    strain_xx = grad_x[:, 0]
    strain_zz = grad_z[:, 1]
    strain_xz = grad_z[:, 0] + grad_x[:, 1]
    stress_xx = waves[:, 2] + signs * (coefs[0] * strain_xx + coefs[1] * strain_zz + coefs[2] * strain_xz)
    stress_zz = waves[:, 3] + signs * (coefs[1] * strain_xx + coefs[3] * strain_zz + coefs[4] * strain_xz)
    stress_xz = waves[:, 4] + signs * (coefs[2] * strain_xx + coefs[4] * strain_zz + coefs[5] * strain_xz)
    updated = jnp.stack([velocity[:, 0], velocity[:, 1], stress_xx, stress_zz, stress_xz], axis=1) * profile
    pressure = updated[:, 2] + updated[:, 3]
    return updated, pressure[0] * pressure[1] * (1.0 / STEPS)


def reference(waves, traces, rec_tile, rec_col, offsets, directory, model_store):
    signs = jnp.array([-1.0, 1.0], dtype=jnp.float32).reshape(2, 1, 1)
    width = NXA
    profile = damping(jnp.arange(width, dtype=jnp.int32), width, NZ)
    cells = jnp.arange(width, dtype=jnp.int32)

    def one_shot(items):
        state, trace_rows, tiles, columns, offset = items
        slot = directory[offset].astype(jnp.int32)
        coefs = lax.dynamic_index_in_dim(model_store, slot, 1, keepdims=False).astype(jnp.float32)
        position = tiles[:, 0] * CX + columns
        place = (position[:, None] == cells[None, :]).astype(jnp.float32)
        inject = jnp.dot(trace_rows, place, precision=lax.Precision.HIGHEST)
        zero_left = jnp.zeros((2, 3, 1, NZ), jnp.float32)
        zero_right = jnp.zeros((2, 2, 1, NZ), jnp.float32)

        def turn(carry, row):
            fields, image = carry
            fields = velocity_update(fields, coefs, signs, zero_left, row)
            fields, term = stress_update(fields, coefs, signs, zero_right, profile)
            return (fields, image + term), None

        start = (state, jnp.zeros((width, NZ), jnp.float32))
        (fields, image), unused = lax.scan(turn, start, inject)
        return fields, image

    waves_out, images = lax.map(one_shot, (waves, traces, rec_tile, rec_col, offsets))
    image_stack = jnp.zeros((NBLK, width, NZ), jnp.float32).at[offsets].add(images)
    return waves_out, image_stack
```

```python
import functools

import jax
import jax.numpy as jnp
from jax import lax
from jax.experimental import pallas as pl
from jax.experimental.pallas import tpu as pltpu
from jax.sharding import PartitionSpec as P

STEPS = 16
PML = 16
REC_DEPTH = 24
damping_peak = 0.2

COLS = 8
TILES = 32
WIDE = 3 * COLS
PHASE = 8
ROWS = 32
VMEM_LIMIT = 56 * 1024 * 1024


def pick_kernel(offsets_ref, directory_ref, store_ref, out_ref):
    shots = out_ref.shape[0]

    def one(shot, _):
        slot = directory_ref[offsets_ref[shot]]
        for entry in range(7):
            out_ref[shot, entry] = store_ref[entry, slot]
        return 0

    lax.fori_loop(0, shots, one, 0)


def row_of(tile):
    return (tile % 4) * 8 + tile // 4


def iota8(axis):
    return lax.broadcasted_iota(jnp.int32, (8, 128), axis)


def lane_index():
    return lax.broadcasted_iota(jnp.int32, (ROWS, 128), 1)


def from_below(v, lane, sub):
    r = pltpu.roll(v, 1, 1)
    wrap = jnp.where(sub == 0, 0.0, pltpu.roll(r[24:32], 1, 0))
    return jnp.where(lane == 0, jnp.concatenate([wrap, r[0:24]], axis=0), r)


def from_above(v, lane, sub):
    r = pltpu.roll(v, 127, 1)
    wrap = jnp.where(sub == 7, 0.0, pltpu.roll(r[0:8], 7, 0))
    return jnp.where(lane == 127, jnp.concatenate([r[8:32], wrap], axis=0), r)


def advance(state, coef, image, inject_ref, first_step):
    lane = lane_index()
    sub = iota8(0)
    spot = jnp.where((iota8(0) == 0) & (iota8(1) == REC_DEPTH), 1.0, 0.0)

    def at(column):
        return pl.ds(pl.multiple_of(column * ROWS, ROWS), ROWS)

    def stress_at(w, i):
        return tuple(state[5 * w + q, at(i), :] for q in (2, 3, 4))

    def velocity(w, i, old, step):
        sxx, szz, sxz = here = stress_at(w, i)
        sxx_l, szz_l, sxz_l = old
        half_b = coef[6, at(i), :]
        d, s = sxx - sxx_l, sxz + sxz_l
        gx = half_b * (d + s + from_below(d - s, lane, sub))
        d, s = sxz - sxz_l, szz + szz_l
        gz = half_b * (d + s + from_below(d - s, lane, sub))
        vx = state[5 * w, at(i), :]
        vz = state[5 * w + 1, at(i), :]
        if w == 0:
            vx, vz = vx - gx, vz - gz
        else:
            vx, vz = vx + gx, vz + gz
            add = inject_ref[first_step + step - 1, i]
            vz = jnp.concatenate([vz[0:8] + add * spot, vz[8:32]], axis=0)
        damp = coef[7, at(i), :]
        state[5 * w, at(i), :] = vx * damp
        state[5 * w + 1, at(i), :] = vz * damp
        vx_z = from_above(vx, lane, sub)
        vz_z = from_above(vz, lane, sub)
        px, mx = vx + vx_z, vx_z - vx
        pz, mz = vz + vz_z, vz_z - vz
        return here, (px, mz, mx - pz), mx + pz

    def stress(w, i, old, left, here, g2):
        exx = here[0] - left[0]
        ezz = here[1] + left[1]
        gxz = left[2] + g2
        c = [coef[q, at(i), :] for q in range(6)]
        damp = coef[7, at(i), :]
        txx = c[0] * exx + c[1] * ezz + c[2] * gxz
        tzz = c[1] * exx + c[3] * ezz + c[4] * gxz
        txz = c[2] * exx + c[4] * ezz + c[5] * gxz
        sxx, szz, sxz = old
        if w == 0:
            new = (sxx - txx, szz - tzz, sxz - txz)
        else:
            new = (sxx + txx, szz + tzz, sxz + txz)
        new = tuple(v * damp for v in new)
        for q in range(3):
            state[5 * w + 2 + q, at(i), :] = new[q]
        return new[0] + new[1]

    def one_step(step, _):
        carry = []
        for w in range(2):
            here, left, _ = velocity(w, step, stress_at(w, step - 1), step)
            carry.append((here, left))

        def column(i, carry):
            after, pressure = [], []
            for w in range(2):
                old, left = carry[w]
                here, now, g2 = velocity(w, i, old, step)
                pressure.append(stress(w, i - 1, old, left, now, g2))
                after.append((here, now))
            image[at(i - 1), :] += pressure[0] * pressure[1]
            return tuple(after)

        lax.fori_loop(step + 1, WIDE - step + 1, column, tuple(carry))
        return 0

    lax.fori_loop(1, PHASE + 1, one_step, 0)


def first_kernel(
    slab_ref,
    inject_ref,
    left_ref,
    own_ref,
    right_ref,
    coef_left_ref,
    coef_own_ref,
    coef_right_ref,
    state_out,
    coef,
    image_out,
    state,
    image,
):
    for part, (waves, store) in enumerate(
        ((left_ref, coef_left_ref), (own_ref, coef_own_ref), (right_ref, coef_right_ref))
    ):
        base = part * COLS * ROWS
        for tile in range(TILES):
            rows = pl.ds(base + row_of(tile), COLS, stride=ROWS)
            lanes = pl.ds(tile * 128, 128)
            for q in range(10):
                state[q, rows, :] = waves[q, :, lanes]
            for q in range(7):
                coef[q, rows, :] = 0.5 * store[tile, q].astype(jnp.float32)

    row = lax.broadcasted_iota(jnp.int32, (ROWS, 128), 0)
    z = (row % 8) * 512 + (row // 8) * 128 + lane_index()
    depth = ROWS * 128
    wide_z = jnp.maximum(jnp.maximum(PML - z, z - (depth - 1 - PML)), 0).astype(jnp.float32) / PML
    square_z = wide_z * wide_z

    def profile(i, _):
        x = (slab_ref[0] - 1) * COLS + i
        total = slab_ref[1] * COLS
        wide_x = jnp.maximum(jnp.maximum(PML - x, x - (total - 1 - PML)), 0).astype(jnp.float32) * (1.0 / PML)
        coef[7, pl.ds(pl.multiple_of(i * ROWS, ROWS), ROWS), :] = 1.0 - damping_peak * (wide_x * wide_x + square_z)
        return 0

    lax.fori_loop(0, WIDE, profile, 0)
    image[...] = jnp.zeros_like(image)
    advance(state, coef, image, inject_ref, 0)
    mid = pl.ds(COLS * ROWS, COLS * ROWS)
    for q in range(10):
        state_out[q] = state[q, mid, :]
    image_out[...] = image[mid, :]


def second_kernel(
    inject_ref, left_ref, own_ref, right_ref, coef, image_in, waves_out, image_out, state, image
):
    size = COLS * ROWS
    for part, waves in enumerate((left_ref, own_ref, right_ref)):
        for q in range(10):
            state[q, pl.ds(part * size, size), :] = waves[q]
    image[...] = jnp.zeros_like(image)
    image[pl.ds(size, size), :] = image_in[...]
    advance(state, coef, image, inject_ref, PHASE)
    for tile in range(TILES):
        rows = pl.ds(size + row_of(tile), COLS, stride=ROWS)
        for q in range(10):
            waves_out[q, :, pl.ds(tile * 128, 128)] = state[q, rows, :]
        image_out[tile] = image[rows, :] * (1.0 / STEPS)


def stack_kernel(offsets_ref, pieces_ref, out_ref):
    out_ref[...] = jnp.zeros_like(out_ref)

    def one(shot, _):
        out_ref[offsets_ref[shot]] += pieces_ref[shot]
        return 0

    lax.fori_loop(0, pieces_ref.shape[0], one, 0)


VMEM = pl.BlockSpec(memory_space=pltpu.VMEM)
SMEM = pl.BlockSpec(memory_space=pltpu.SMEM)
PARAMS = pltpu.CompilerParams(vmem_limit_bytes=VMEM_LIMIT)


def shape(*dims, dtype=jnp.float32):
    return jax.ShapeDtypeStruct(dims, dtype)


def neighbours(block, axis):
    count = lax.axis_size(axis)
    up = [(i, i + 1) for i in range(count - 1)]
    down = [(i + 1, i) for i in range(count - 1)]
    return lax.ppermute(block, axis, up), lax.ppermute(block, axis, down)


def injection(traces, rec_tile, rec_col, slabs):
    cell = rec_tile[0, :, 0] * COLS + rec_col[0]
    window = jnp.arange(slabs, dtype=jnp.int32)[:, None] * COLS - COLS + jnp.arange(WIDE, dtype=jnp.int32)[None, :]
    place = (cell[:, None] == window.reshape(1, -1)).astype(jnp.float32)
    part = jnp.dot(traces[0], place, precision=lax.Precision.HIGHEST)
    part = part.reshape(STEPS, slabs, WIDE).transpose(1, 0, 2).reshape(slabs, STEPS * WIDE // 128, 128)
    part = lax.all_to_all(part, "slab", split_axis=0, concat_axis=0, tiled=True)
    return part.sum(axis=0).reshape(STEPS, WIDE)


def local(waves, traces, rec_tile, rec_col, offsets, directory, model_store):
    slabs = lax.axis_size("slab")
    shots = lax.axis_size("shot")
    depth = waves.shape[4]
    own = waves.reshape(10, COLS, depth)
    left, right = neighbours(own, "slab")

    picked = pl.pallas_call(
        pick_kernel,
        out_shape=shape(shots, 7, COLS, 128, dtype=jnp.bfloat16),
        in_specs=[SMEM, SMEM, VMEM],
        out_specs=VMEM,
        compiler_params=PARAMS,
    )(offsets, directory, model_store)
    coef_own = lax.all_to_all(picked, "shot", split_axis=0, concat_axis=0, tiled=True)
    coef_left, coef_right = neighbours(coef_own, "slab")
    inject = injection(traces, rec_tile, rec_col, slabs)

    place = jnp.stack([lax.axis_index("slab"), jnp.int32(slabs)]).astype(jnp.int32)
    own_rows = COLS * ROWS
    all_rows = WIDE * ROWS
    state, coef, image = pl.pallas_call(
        first_kernel,
        out_shape=(shape(10, own_rows, 128), shape(8, all_rows, 128), shape(own_rows, 128)),
        in_specs=[SMEM, SMEM] + [VMEM] * 6,
        out_specs=(VMEM,) * 3,
        scratch_shapes=[pltpu.VMEM((10, all_rows, 128), jnp.float32), pltpu.VMEM((all_rows, 128), jnp.float32)],
        compiler_params=PARAMS,
    )(place, inject, left, own, right, coef_left, coef_own, coef_right)
    state_left, state_right = neighbours(state, "slab")
    waves_out, pieces = pl.pallas_call(
        second_kernel,
        out_shape=(shape(10, COLS, depth), shape(TILES, COLS, 128)),
        in_specs=[SMEM] + [VMEM] * 5,
        out_specs=(VMEM,) * 2,
        scratch_shapes=[pltpu.VMEM((10, all_rows, 128), jnp.float32), pltpu.VMEM((all_rows, 128), jnp.float32)],
        compiler_params=PARAMS,
    )(inject, state_left, state, state_right, coef, image)
    pieces = lax.all_to_all(pieces, "shot", split_axis=0, concat_axis=0, tiled=True)
    stacked = pl.pallas_call(
        stack_kernel,
        out_shape=shape(model_store.shape[1], COLS, 128),
        in_specs=[SMEM, VMEM],
        out_specs=VMEM,
        compiler_params=PARAMS,
    )(offsets, pieces)
    return waves_out.reshape(waves.shape), stacked


def solution(mesh):
    placed = (
        P("shot", None, None, "slab", None),
        P("shot", None, "slab"),
        P("shot", "slab", None),
        P("shot", "slab"),
        P(),
        P(),
        P(None, None, "slab", "shot"),
    )
    return jax.shard_map(
        local,
        mesh=mesh,
        in_specs=placed,
        out_specs=(P("shot", None, None, "slab", None), P(None, "slab", "shot")),
        check_vma=False,
    )
```

```python
import functools

import jax
import jax.numpy as jnp
from jax import lax
from jax.experimental import pallas as pl
from jax.experimental.pallas import tpu as pltpu
from jax.sharding import PartitionSpec as P

STEPS = 16
PML = 16
REC_DEPTH = 24
damping_peak = 0.2

COLS = 8
TILES = 32
WIDE = 3 * COLS
PHASE = 8
PAD = 4
HELD = 36
GRADS, PARTS, PLANES = 10, 14, 22
ROWS = 32
VMEM_LIMIT = 40 * 1024 * 1024


def pick_kernel(offsets_ref, directory_ref, store_ref, out_ref):
    shots = out_ref.shape[0]

    def one(shot, _):
        slot = directory_ref[offsets_ref[shot]]
        for entry in range(7):
            out_ref[shot, entry] = store_ref[entry, slot]
        return 0

    lax.fori_loop(0, shots, one, 0)


def row_of(tile):
    return (tile % 4) * 8 + tile // 4


def iota8(axis):
    return lax.broadcasted_iota(jnp.int32, (8, 128), axis)


def lane_index():
    return lax.broadcasted_iota(jnp.int32, (ROWS, 128), 1)


def from_below(v, lane, sub):
    r = pltpu.roll(v, 1, 1)
    wrap = jnp.where(sub == 0, 0.0, pltpu.roll(r[24:32], 1, 0))
    return jnp.where(lane == 0, jnp.concatenate([wrap, r[0:24]], axis=0), r)


def from_above(v, lane, sub):
    r = pltpu.roll(v, 127, 1)
    wrap = jnp.where(sub == 7, 0.0, pltpu.roll(r[0:8], 7, 0))
    return jnp.where(lane == 127, jnp.concatenate([r[8:32], wrap], axis=0), r)


def advance(state, coef, image, inject_ref, first_step):
    lane = lane_index()
    sub = iota8(0)
    spot = jnp.where((iota8(0) == 0) & (iota8(1) == REC_DEPTH), 1.0, 0.0)

    def at(base, k):
        return pl.ds(pl.multiple_of(base + k * ROWS, ROWS), ROWS)

    def stress_at(w, base, k):
        return tuple(state[5 * w + q, at(base, k), :] for q in (2, 3, 4))

    def gradients(base, ks):
        for w in range(2):
            left = stress_at(w, base, ks[0] - 1)
            for k in ks:
                here = stress_at(w, base, k)
                d, s = here[0] - left[0], here[2] + left[2]
                state[GRADS + 2 * w, at(base, k), :] = d + s + from_below(d - s, lane, sub)
                d, s = here[2] - left[2], here[1] + left[1]
                state[GRADS + 2 * w + 1, at(base, k), :] = d + s + from_below(d - s, lane, sub)
                left = here

    def velocities(a, base, ks, step):
        for k in ks:
            half_b = coef[6, at(base, k), :]
            damp = coef[7, at(base, k), :]
            for w in range(2):
                gx = half_b * state[GRADS + 2 * w, at(base, k), :]
                gz = half_b * state[GRADS + 2 * w + 1, at(base, k), :]
                vx = state[5 * w, at(base, k), :]
                vz = state[5 * w + 1, at(base, k), :]
                if w == 0:
                    vx, vz = vx - gx, vz - gz
                else:
                    vx, vz = vx + gx, vz + gz
                    add = inject_ref[first_step + step - 1, a + k]
                    vz = jnp.concatenate([vz[0:8] + add * spot, vz[8:32]], axis=0)
                state[5 * w, at(base, k), :] = vx * damp
                state[5 * w + 1, at(base, k), :] = vz * damp
                vx_z = from_above(vx, lane, sub)
                vz_z = from_above(vz, lane, sub)
                mx, pz = vx_z - vx, vz + vz_z
                state[PARTS + 4 * w, at(base, k), :] = vx + vx_z
                state[PARTS + 4 * w + 1, at(base, k), :] = vz_z - vz
                state[PARTS + 4 * w + 2, at(base, k), :] = mx - pz
                state[PARTS + 4 * w + 3, at(base, k), :] = mx + pz

    def stresses(base, ks):
        for k in ks:
            c = [coef[q, at(base, k), :] for q in range(6)]
            damp = coef[7, at(base, k), :]
            pressure = []
            for w in range(2):
                exx = state[PARTS + 4 * w, at(base, k + 1), :] - state[PARTS + 4 * w, at(base, k), :]
                ezz = state[PARTS + 4 * w + 1, at(base, k + 1), :] + state[PARTS + 4 * w + 1, at(base, k), :]
                gxz = state[PARTS + 4 * w + 3, at(base, k + 1), :] + state[PARTS + 4 * w + 2, at(base, k), :]
                txx = c[0] * exx + c[1] * ezz + c[2] * gxz
                tzz = c[1] * exx + c[3] * ezz + c[4] * gxz
                txz = c[2] * exx + c[4] * ezz + c[5] * gxz
                sxx, szz, sxz = stress_at(w, base, k)
                if w == 0:
                    new = (sxx - txx, szz - tzz, sxz - txz)
                else:
                    new = (sxx + txx, szz + tzz, sxz + txz)
                new = tuple(v * damp for v in new)
                for q in range(3):
                    state[5 * w + 2 + q, at(base, k), :] = new[q]
                pressure.append(new[0] + new[1])
            image[at(base, k), :] += pressure[0] * pressure[1]

    def one_step(step, _):
        start = pl.multiple_of((step + PAD) * ROWS, ROWS)
        gradients(start, (0, 1))

        def turn(j, _):
            a = step + 2 * j
            base = pl.multiple_of((a + PAD) * ROWS, ROWS)
            velocities(a, base, (0, 1), step)
            gradients(base, (2, 3))
            stresses(base, (-3, -2))
            return 0

        lax.fori_loop(0, PHASE + 6 - step, turn, 0)
        return 0

    lax.fori_loop(1, PHASE + 1, one_step, 0)


def window(part):
    return pl.ds((PAD + part * COLS) * ROWS, COLS * ROWS)


def waves_kernel(left_ref, own_ref, right_ref, out_ref):
    for part, waves in enumerate((left_ref, own_ref, right_ref)):
        for tile in range(TILES):
            rows = pl.ds(part * COLS * ROWS + row_of(tile), COLS, stride=ROWS)
            for q in range(10):
                out_ref[q, rows, :] = waves[q, :, pl.ds(tile * 128, 128)]


def inject_kernel(traces_ref, tile_ref, col_ref, out_ref):
    cell = tile_ref[...] * COLS + col_ref[...]
    column = lax.broadcasted_iota(jnp.int32, (128, 128), 0)
    for slab in range(out_ref.shape[0]):
        hit = (cell == column + (slab - 1) * COLS) & (column < WIDE)
        out_ref[slab] = lax.dot_general(
            traces_ref[...],
            jnp.where(hit, 1.0, 0.0),
            (((1,), (1,)), ((), ())),
            precision=lax.Precision.HIGHEST,
            preferred_element_type=jnp.float32,
        )


def first_kernel(
    slabs,
    slab_ref,
    inject_ref,
    waves_ref,
    coef_left_ref,
    coef_own_ref,
    coef_right_ref,
    state_out,
    coef_out,
    image_out,
    state,
    coef,
    image,
    sem,
):
    all_rows = pl.ds(PAD * ROWS, WIDE * ROWS)
    copy = pltpu.make_async_copy(waves_ref, state.at[pl.ds(0, 10), all_rows, :], sem)
    copy.start()
    for part, store in enumerate((coef_left_ref, coef_own_ref, coef_right_ref)):
        base = (PAD + part * COLS) * ROWS
        for tile in range(TILES):
            rows = pl.ds(base + row_of(tile), COLS, stride=ROWS)
            for q in range(7):
                coef[q, rows, :] = 0.5 * store[tile, q].astype(jnp.float32)

    row = lax.broadcasted_iota(jnp.int32, (ROWS, 128), 0)
    z = (row % 8) * 512 + (row // 8) * 128 + lane_index()
    depth = ROWS * 128
    wide_z = jnp.maximum(jnp.maximum(PML - z, z - (depth - 1 - PML)), 0).astype(jnp.float32) / PML
    square_z = wide_z * wide_z
    first = (slab_ref[0] - 1) * COLS

    def profile(i, _):
        x = first + i
        last = slabs * COLS - 1 - PML
        wide_x = jnp.maximum(jnp.maximum(PML - x, x - last), 0).astype(jnp.float32) * (1.0 / PML)
        rows = pl.ds(pl.multiple_of((i + PAD) * ROWS, ROWS), ROWS)
        coef[7, rows, :] = 1.0 - damping_peak * (wide_x * wide_x + square_z)
        return 0

    lax.fori_loop(0, WIDE, profile, 0)
    image[...] = jnp.zeros_like(image)
    copy.wait()
    advance(state, coef, image, inject_ref, 0)
    for q in range(10):
        state_out[q] = state[q, window(1), :]
    for q in range(8):
        coef_out[q] = coef[q, all_rows, :]
    image_out[...] = image[window(1), :]


def second_kernel(
    inject_ref,
    left_ref,
    own_ref,
    right_ref,
    coef_ref,
    image_in,
    waves_out,
    image_out,
    state,
    coef,
    image,
    sems,
):
    copies = [
        pltpu.make_async_copy(ref, state.at[pl.ds(0, 10), window(part), :], sems.at[part])
        for part, ref in enumerate((left_ref, own_ref, right_ref))
    ]
    copies.append(pltpu.make_async_copy(coef_ref, coef.at[:, pl.ds(PAD * ROWS, WIDE * ROWS), :], sems.at[3]))
    for copy in copies:
        copy.start()
    image[...] = jnp.zeros_like(image)
    image[window(1), :] = image_in[...]
    for copy in copies:
        copy.wait()
    advance(state, coef, image, inject_ref, PHASE)
    for tile in range(TILES):
        rows = pl.ds((PAD + COLS) * ROWS + row_of(tile), COLS, stride=ROWS)
        for q in range(10):
            waves_out[q, :, pl.ds(tile * 128, 128)] = state[q, rows, :]
        image_out[tile] = image[rows, :] * (1.0 / STEPS)


def stack_kernel(offsets_ref, pieces_ref, out_ref):
    out_ref[...] = jnp.zeros_like(out_ref)

    def one(shot, _):
        out_ref[offsets_ref[shot]] += pieces_ref[shot]
        return 0

    lax.fori_loop(0, pieces_ref.shape[0], one, 0)


VMEM = pl.BlockSpec(memory_space=pltpu.VMEM)
ANY = pl.BlockSpec(memory_space=pl.ANY)
SMEM = pl.BlockSpec(memory_space=pltpu.SMEM)
PARAMS = pltpu.CompilerParams(vmem_limit_bytes=VMEM_LIMIT)


def shape(*dims, dtype=jnp.float32):
    return jax.ShapeDtypeStruct(dims, dtype)


def neighbours(block, axis):
    count = lax.axis_size(axis)
    up = [(i, i + 1) for i in range(count - 1)]
    down = [(i + 1, i) for i in range(count - 1)]
    return lax.ppermute(block, axis, up), lax.ppermute(block, axis, down)


def scratch(copies):
    held = HELD * ROWS
    return [
        pltpu.VMEM((PLANES, held, 128), jnp.float32),
        pltpu.VMEM((8, held, 128), jnp.float32),
        pltpu.VMEM((held, 128), jnp.float32),
        pltpu.SemaphoreType.DMA((copies,)) if copies > 1 else pltpu.SemaphoreType.DMA,
    ]


def local(waves, traces, rec_tile, rec_col, offsets, directory, model_store):
    slabs = lax.axis_size("slab")
    shots = lax.axis_size("shot")
    depth = waves.shape[4]
    own = waves.reshape(10, COLS, depth)
    own_rows = COLS * ROWS
    all_rows = WIDE * ROWS

    picked = pl.pallas_call(
        pick_kernel,
        out_shape=shape(shots, 7, COLS, 128, dtype=jnp.bfloat16),
        in_specs=[SMEM, SMEM, VMEM],
        out_specs=VMEM,
        compiler_params=PARAMS,
    )(offsets, directory, model_store)
    coef_own = lax.all_to_all(picked, "shot", split_axis=0, concat_axis=0, tiled=True)

    left, right = neighbours(own, "slab")
    adds = pl.pallas_call(
        inject_kernel,
        out_shape=shape(slabs, STEPS, 128),
        in_specs=[VMEM] * 3,
        out_specs=VMEM,
        compiler_params=PARAMS,
    )(traces[0], rec_tile.reshape(1, -1), rec_col)
    inject = lax.all_to_all(adds, "slab", split_axis=0, concat_axis=0, tiled=True).sum(axis=0)
    waves_in = pl.pallas_call(
        waves_kernel,
        out_shape=shape(10, all_rows, 128),
        in_specs=[VMEM] * 3,
        out_specs=VMEM,
        compiler_params=PARAMS,
        cost_estimate=pl.CostEstimate(flops=0, bytes_accessed=8 << 20, transcendentals=0),
    )(left, own, right)

    coef_own, inject = lax.optimization_barrier((coef_own, inject))
    coef_left, coef_right = neighbours(coef_own, "slab")
    state, coef, image = pl.pallas_call(
        functools.partial(first_kernel, slabs),
        out_shape=(shape(10, own_rows, 128), shape(8, all_rows, 128), shape(own_rows, 128)),
        in_specs=[SMEM, SMEM, ANY] + [VMEM] * 3,
        out_specs=(VMEM,) * 3,
        scratch_shapes=scratch(1),
        compiler_params=PARAMS,
    )(lax.axis_index("slab").astype(jnp.int32).reshape(1), inject, waves_in, coef_left, coef_own, coef_right)
    state_left, state_right = neighbours(state, "slab")
    waves_out, pieces = pl.pallas_call(
        second_kernel,
        out_shape=(shape(10, COLS, depth), shape(TILES, COLS, 128)),
        in_specs=[SMEM] + [ANY] * 4 + [VMEM],
        out_specs=(VMEM,) * 2,
        scratch_shapes=scratch(4),
        compiler_params=PARAMS,
    )(inject, state_left, state, state_right, coef, image)
    pieces = lax.all_to_all(pieces, "shot", split_axis=0, concat_axis=0, tiled=True)
    stacked = pl.pallas_call(
        stack_kernel,
        out_shape=shape(model_store.shape[1], COLS, 128),
        in_specs=[SMEM, VMEM],
        out_specs=VMEM,
        compiler_params=PARAMS,
    )(offsets, pieces)
    return waves_out.reshape(waves.shape), stacked


def solution(mesh):
    placed = (
        P("shot", None, None, "slab", None),
        P("shot", None, "slab"),
        P("shot", "slab", None),
        P("shot", "slab"),
        P(),
        P(),
        P(None, None, "slab", "shot"),
    )
    return jax.shard_map(
        local,
        mesh=mesh,
        in_specs=placed,
        out_specs=(P("shot", None, None, "slab", None), P(None, "slab", "shot")),
        check_vma=False,
    )
```

```python
import functools

import jax
import jax.numpy as jnp
from jax import lax
from jax.experimental import pallas as pl
from jax.experimental.pallas import tpu as pltpu
from jax.sharding import PartitionSpec as P

STEPS = 16
PML = 16
REC_DEPTH = 24
damping_peak = 0.2

COLS = 8
TILES = 32
WIDE = 3 * COLS
PHASE = 8
PAD = 4
HELD = 36
GRADS, PARTS, PLANES = 10, 14, 22
ROWS = 32
VMEM_LIMIT = 32 * 1024 * 1024


def pick_kernel(offsets_ref, directory_ref, store_ref, out_ref):
    shots = out_ref.shape[0]

    def one(shot, _):
        slot = directory_ref[offsets_ref[shot]]
        for entry in range(7):
            out_ref[shot, entry] = store_ref[entry, slot]
        return 0

    lax.fori_loop(0, shots, one, 0)


def row_of(tile):
    return (tile % 4) * 8 + tile // 4


def iota8(axis):
    return lax.broadcasted_iota(jnp.int32, (8, 128), axis)


def lane_index():
    return lax.broadcasted_iota(jnp.int32, (ROWS, 128), 1)


def from_below(v, lane, sub):
    r = pltpu.roll(v, 1, 1)
    wrap = jnp.where(sub == 0, 0.0, pltpu.roll(r[24:32], 1, 0))
    return jnp.where(lane == 0, jnp.concatenate([wrap, r[0:24]], axis=0), r)


def from_above(v, lane, sub):
    r = pltpu.roll(v, 127, 1)
    wrap = jnp.where(sub == 7, 0.0, pltpu.roll(r[0:8], 7, 0))
    return jnp.where(lane == 127, jnp.concatenate([r[8:32], wrap], axis=0), r)


def advance(state, coef, image, slab, inject_ref, first_step):
    lane = lane_index()
    sub = iota8(0)
    spot = jnp.where((iota8(0) == 0) & (iota8(1) == REC_DEPTH), 1.0, 0.0)

    def at(base, k):
        return pl.ds(pl.multiple_of(base + k * ROWS, ROWS), ROWS)

    def stress_at(w, base, k):
        return tuple(state[5 * w + q, at(base, k), :] for q in (2, 3, 4))

    def gradients(base, ks):
        for w in range(2):
            left = stress_at(w, base, ks[0] - 1)
            for k in ks:
                here = stress_at(w, base, k)
                d, s = here[0] - left[0], here[2] + left[2]
                state[GRADS + 2 * w, at(base, k), :] = d + s + from_below(d - s, lane, sub)
                d, s = here[2] - left[2], here[1] + left[1]
                state[GRADS + 2 * w + 1, at(base, k), :] = d + s + from_below(d - s, lane, sub)
                left = here

    def velocities(a, base, ks, step):
        for k in ks:
            half_b = coef[6, at(base, k), :]
            damp = coef[7, at(base, k), :]
            for w in range(2):
                gx = half_b * state[GRADS + 2 * w, at(base, k), :]
                gz = half_b * state[GRADS + 2 * w + 1, at(base, k), :]
                vx = state[5 * w, at(base, k), :]
                vz = state[5 * w + 1, at(base, k), :]
                if w == 0:
                    vx, vz = vx - gx, vz - gz
                else:
                    vx, vz = vx + gx, vz + gz
                    add = inject_ref[first_step + step - 1, (slab + 1) * COLS + a + k]
                    vz = jnp.concatenate([vz[0:8] + add * spot, vz[8:32]], axis=0)
                state[5 * w, at(base, k), :] = vx * damp
                state[5 * w + 1, at(base, k), :] = vz * damp
                vx_z = from_above(vx, lane, sub)
                vz_z = from_above(vz, lane, sub)
                mx, pz = vx_z - vx, vz + vz_z
                state[PARTS + 4 * w, at(base, k), :] = vx + vx_z
                state[PARTS + 4 * w + 1, at(base, k), :] = vz_z - vz
                state[PARTS + 4 * w + 2, at(base, k), :] = mx - pz
                state[PARTS + 4 * w + 3, at(base, k), :] = mx + pz

    def stresses(base, ks):
        for k in ks:
            c = [coef[q, at(base, k), :] for q in range(6)]
            damp = coef[7, at(base, k), :]
            pressure = []
            for w in range(2):
                exx = state[PARTS + 4 * w, at(base, k + 1), :] - state[PARTS + 4 * w, at(base, k), :]
                ezz = state[PARTS + 4 * w + 1, at(base, k + 1), :] + state[PARTS + 4 * w + 1, at(base, k), :]
                gxz = state[PARTS + 4 * w + 3, at(base, k + 1), :] + state[PARTS + 4 * w + 2, at(base, k), :]
                txx = c[0] * exx + c[1] * ezz + c[2] * gxz
                tzz = c[1] * exx + c[3] * ezz + c[4] * gxz
                txz = c[2] * exx + c[4] * ezz + c[5] * gxz
                sxx, szz, sxz = stress_at(w, base, k)
                if w == 0:
                    new = (sxx - txx, szz - tzz, sxz - txz)
                else:
                    new = (sxx + txx, szz + tzz, sxz + txz)
                new = tuple(v * damp for v in new)
                for q in range(3):
                    state[5 * w + 2 + q, at(base, k), :] = new[q]
                pressure.append(new[0] + new[1])
            image[at(base, k), :] += pressure[0] * pressure[1]

    def one_step(step, _):
        start = pl.multiple_of((step + PAD) * ROWS, ROWS)
        gradients(start, (0, 1))

        def turn(j, _):
            a = step + 2 * j
            base = pl.multiple_of((a + PAD) * ROWS, ROWS)
            velocities(a, base, (0, 1), step)
            gradients(base, (2, 3))
            stresses(base, (-3, -2))
            return 0

        lax.fori_loop(0, PHASE + 6 - step, turn, 0)
        return 0

    lax.fori_loop(1, PHASE + 1, one_step, 0)


def window(part):
    return pl.ds((PAD + part * COLS) * ROWS, COLS * ROWS)


def waves_kernel(left_ref, own_ref, right_ref, out_ref):
    for part, waves in enumerate((left_ref, own_ref, right_ref)):
        for tile in range(TILES):
            rows = pl.ds(part * COLS * ROWS + row_of(tile), COLS, stride=ROWS)
            for q in range(10):
                out_ref[q, rows, :] = waves[q, :, pl.ds(tile * 128, 128)]


def inject_kernel(traces_ref, tile_ref, col_ref, out_ref):
    cell = tile_ref[...] * COLS + col_ref[...]
    lane = lax.broadcasted_iota(jnp.int32, (128, 128), 0)
    out_ref[...] = lax.dot_general(
        traces_ref[...],
        jnp.where(cell + 2 * COLS == lane, 1.0, 0.0),
        (((1,), (1,)), ((), ())),
        precision=lax.Precision.HIGHEST,
        preferred_element_type=jnp.float32,
    )


def first_kernel(
    slabs,
    slab_ref,
    inject_ref,
    waves_ref,
    coef_left_ref,
    coef_own_ref,
    coef_right_ref,
    state_out,
    coef,
    image_out,
    state,
    image,
    sem,
):
    all_rows = pl.ds(PAD * ROWS, WIDE * ROWS)
    copy = pltpu.make_async_copy(waves_ref, state.at[pl.ds(0, 10), all_rows, :], sem)
    copy.start()
    for part, store in enumerate((coef_left_ref, coef_own_ref, coef_right_ref)):
        base = (PAD + part * COLS) * ROWS
        for tile in range(TILES):
            rows = pl.ds(base + row_of(tile), COLS, stride=ROWS)
            for q in range(7):
                coef[q, rows, :] = 0.5 * store[tile, q].astype(jnp.float32)

    row = lax.broadcasted_iota(jnp.int32, (ROWS, 128), 0)
    z = (row % 8) * 512 + (row // 8) * 128 + lane_index()
    depth = ROWS * 128
    wide_z = jnp.maximum(jnp.maximum(PML - z, z - (depth - 1 - PML)), 0).astype(jnp.float32) / PML
    square_z = wide_z * wide_z
    slab = slab_ref[0]
    first = (slab - 1) * COLS

    def profile(i, _):
        x = first + i
        last = slabs * COLS - 1 - PML
        wide_x = jnp.maximum(jnp.maximum(PML - x, x - last), 0).astype(jnp.float32) * (1.0 / PML)
        rows = pl.ds(pl.multiple_of((i + PAD) * ROWS, ROWS), ROWS)
        coef[7, rows, :] = 1.0 - damping_peak * (wide_x * wide_x + square_z)
        return 0

    lax.fori_loop(0, WIDE, profile, 0)
    image[...] = jnp.zeros_like(image)
    copy.wait()
    advance(state, coef, image, slab, inject_ref, 0)
    for q in range(10):
        state_out[q] = state[q, window(1), :]
    image_out[...] = image[window(1), :]


def second_kernel(
    slab_ref,
    inject_ref,
    left_ref,
    own_ref,
    right_ref,
    coef,
    image_in,
    waves_out,
    image_out,
    state,
    image,
    sems,
):
    copies = [
        pltpu.make_async_copy(ref, state.at[pl.ds(0, 10), window(part), :], sems.at[part])
        for part, ref in enumerate((left_ref, own_ref, right_ref))
    ]
    for copy in copies:
        copy.start()
    image[...] = jnp.zeros_like(image)
    image[window(1), :] = image_in[...]
    for copy in copies:
        copy.wait()
    advance(state, coef, image, slab_ref[0], inject_ref, PHASE)
    for tile in range(TILES):
        rows = pl.ds((PAD + COLS) * ROWS + row_of(tile), COLS, stride=ROWS)
        for q in range(10):
            waves_out[q, :, pl.ds(tile * 128, 128)] = state[q, rows, :]
        image_out[tile] = image[rows, :] * (1.0 / STEPS)


def stack_kernel(offsets_ref, pieces_ref, out_ref):
    out_ref[...] = jnp.zeros_like(out_ref)

    def one(shot, _):
        out_ref[offsets_ref[shot]] += pieces_ref[shot]
        return 0

    lax.fori_loop(0, pieces_ref.shape[0], one, 0)


VMEM = pl.BlockSpec(memory_space=pltpu.VMEM)
ANY = pl.BlockSpec(memory_space=pl.ANY)
SMEM = pl.BlockSpec(memory_space=pltpu.SMEM)
PARAMS = pltpu.CompilerParams(vmem_limit_bytes=VMEM_LIMIT)
LARGE = pltpu.CompilerParams(vmem_limit_bytes=56 * 1024 * 1024)


def shape(*dims, dtype=jnp.float32):
    return jax.ShapeDtypeStruct(dims, dtype)


def neighbours(block, axis):
    count = lax.axis_size(axis)
    up = [(i, i + 1) for i in range(count - 1)]
    down = [(i + 1, i) for i in range(count - 1)]
    return lax.ppermute(block, axis, up), lax.ppermute(block, axis, down)


def scratch(copies):
    held = HELD * ROWS
    return [
        pltpu.VMEM((PLANES, held, 128), jnp.float32),
        pltpu.VMEM((held, 128), jnp.float32),
        pltpu.SemaphoreType.DMA((copies,)) if copies > 1 else pltpu.SemaphoreType.DMA,
    ]


def local(waves, traces, rec_tile, rec_col, offsets, directory, model_store):
    slabs = lax.axis_size("slab")
    shots = lax.axis_size("shot")
    depth = waves.shape[4]
    own = waves.reshape(10, COLS, depth)
    own_rows = COLS * ROWS
    all_rows = WIDE * ROWS

    def added(rows, bit):
        partner = [(i, i ^ bit) for i in range(slabs)]
        return rows + lax.ppermute(rows, "slab", partner)

    inject = pl.pallas_call(
        inject_kernel,
        out_shape=shape(STEPS, 128),
        in_specs=[VMEM] * 3,
        out_specs=VMEM,
        compiler_params=LARGE,
    )(traces[0], rec_tile.reshape(1, -1), rec_col)
    inject, store = lax.optimization_barrier((inject, model_store))
    picked = pl.pallas_call(
        pick_kernel,
        out_shape=shape(shots, 7, COLS, 128, dtype=jnp.bfloat16),
        in_specs=[SMEM, SMEM, VMEM],
        out_specs=VMEM,
        compiler_params=LARGE,
    )(offsets, directory, store)
    inject, picked = lax.optimization_barrier((added(added(inject, 1), 2), picked))
    coef_own = lax.all_to_all(picked, "shot", split_axis=0, concat_axis=0, tiled=True)
    inject, own = lax.optimization_barrier((added(inject, 4), own))
    left, right = neighbours(own, "slab")
    waves_in = pl.pallas_call(
        waves_kernel,
        out_shape=shape(10, all_rows, 128),
        in_specs=[VMEM] * 3,
        out_specs=VMEM,
        compiler_params=PARAMS,
        cost_estimate=pl.CostEstimate(flops=0, bytes_accessed=8 << 20, transcendentals=0),
    )(left, own, right)

    slab = lax.axis_index("slab").astype(jnp.int32).reshape(1)
    coef_left, coef_right = neighbours(coef_own, "slab")
    state, coef, image = pl.pallas_call(
        functools.partial(first_kernel, slabs),
        out_shape=(shape(10, own_rows, 128), shape(8, HELD * ROWS, 128), shape(own_rows, 128)),
        in_specs=[SMEM, SMEM, ANY] + [VMEM] * 3,
        out_specs=(VMEM,) * 3,
        scratch_shapes=scratch(1),
        compiler_params=PARAMS,
    )(slab, inject, waves_in, coef_left, coef_own, coef_right)
    state_left, state_right = neighbours(state, "slab")
    waves_out, pieces = pl.pallas_call(
        second_kernel,
        out_shape=(shape(10, COLS, depth), shape(TILES, COLS, 128)),
        in_specs=[SMEM, SMEM] + [ANY] * 3 + [VMEM] * 2,
        out_specs=(VMEM,) * 2,
        scratch_shapes=scratch(3),
        compiler_params=PARAMS,
    )(slab, inject, state_left, state, state_right, coef, image)
    pieces = lax.all_to_all(pieces, "shot", split_axis=0, concat_axis=0, tiled=True)
    stacked = pl.pallas_call(
        stack_kernel,
        out_shape=shape(model_store.shape[1], COLS, 128),
        in_specs=[SMEM, VMEM],
        out_specs=VMEM,
        compiler_params=PARAMS,
    )(offsets, pieces)
    return waves_out.reshape(waves.shape), stacked


def solution(mesh):
    placed = (
        P("shot", None, None, "slab", None),
        P("shot", None, "slab"),
        P("shot", "slab", None),
        P("shot", "slab"),
        P(),
        P(),
        P(None, None, "slab", "shot"),
    )
    return jax.shard_map(
        local,
        mesh=mesh,
        in_specs=placed,
        out_specs=(P("shot", None, None, "slab", None), P(None, "slab", "shot")),
        check_vma=False,
    )
```

```python
import functools

import jax
import jax.numpy as jnp
from jax import lax
from jax.experimental import pallas as pl
from jax.experimental.pallas import tpu as pltpu
from jax.sharding import PartitionSpec as P

STEPS = 16
PML = 16
REC_DEPTH = 24
damping_peak = 0.2

COLS = 8
TILES = 32
WIDE = 3 * COLS
PHASE = 8
PAD = 4
HELD = 36
GRADS, PARTS, PLANES = 10, 14, 22
ROWS = 32
VMEM_LIMIT = 32 * 1024 * 1024


def pick_kernel(offsets_ref, directory_ref, store_ref, out_ref):
    shots = out_ref.shape[0]

    def one(shot, _):
        slot = directory_ref[offsets_ref[shot]]
        for entry in range(7):
            out_ref[shot, entry] = store_ref[entry, slot]
        return 0

    lax.fori_loop(0, shots, one, 0)


def row_of(tile):
    return (tile % 4) * 8 + tile // 4


def iota8(axis):
    return lax.broadcasted_iota(jnp.int32, (8, 128), axis)


def lane_index():
    return lax.broadcasted_iota(jnp.int32, (ROWS, 128), 1)


def from_below(v, lane, sub):
    r = pltpu.roll(v, 1, 1)
    wrap = jnp.where(sub == 0, 0.0, pltpu.roll(r[24:32], 1, 0))
    return jnp.where(lane == 0, jnp.concatenate([wrap, r[0:24]], axis=0), r)


def from_above(v, lane, sub):
    r = pltpu.roll(v, 127, 1)
    wrap = jnp.where(sub == 7, 0.0, pltpu.roll(r[0:8], 7, 0))
    return jnp.where(lane == 127, jnp.concatenate([r[8:32], wrap], axis=0), r)


def advance(state, coef, image, slab, inject_ref, first_step):
    lane = lane_index()
    sub = iota8(0)
    spot = jnp.where((iota8(0) == 0) & (iota8(1) == REC_DEPTH), 1.0, 0.0)

    def at(base, k):
        return pl.ds(pl.multiple_of(base + k * ROWS, ROWS), ROWS)

    def stress_at(w, base, k):
        return tuple(state[5 * w + q, at(base, k), :] for q in (2, 3, 4))

    def gradients(base, ks):
        for w in range(2):
            left = stress_at(w, base, ks[0] - 1)
            for k in ks:
                here = stress_at(w, base, k)
                d, s = here[0] - left[0], here[2] + left[2]
                state[GRADS + 2 * w, at(base, k), :] = d + s + from_below(d - s, lane, sub)
                d, s = here[2] - left[2], here[1] + left[1]
                state[GRADS + 2 * w + 1, at(base, k), :] = d + s + from_below(d - s, lane, sub)
                left = here

    def velocities(a, base, ks, step):
        for k in ks:
            half_b = coef[6, at(base, k), :]
            damp = coef[7, at(base, k), :]
            for w in range(2):
                gx = half_b * state[GRADS + 2 * w, at(base, k), :]
                gz = half_b * state[GRADS + 2 * w + 1, at(base, k), :]
                vx = state[5 * w, at(base, k), :]
                vz = state[5 * w + 1, at(base, k), :]
                if w == 0:
                    vx, vz = vx - gx, vz - gz
                else:
                    vx, vz = vx + gx, vz + gz
                    add = inject_ref[first_step + step - 1, (slab + 1) * COLS + a + k]
                    vz = jnp.concatenate([vz[0:8] + add * spot, vz[8:32]], axis=0)
                state[5 * w, at(base, k), :] = vx * damp
                state[5 * w + 1, at(base, k), :] = vz * damp
                vx_z = from_above(vx, lane, sub)
                vz_z = from_above(vz, lane, sub)
                mx, pz = vx_z - vx, vz + vz_z
                state[PARTS + 4 * w, at(base, k), :] = vx + vx_z
                state[PARTS + 4 * w + 1, at(base, k), :] = vz_z - vz
                state[PARTS + 4 * w + 2, at(base, k), :] = mx - pz
                state[PARTS + 4 * w + 3, at(base, k), :] = mx + pz

    def stresses(base, ks):
        for k in ks:
            c = [coef[q, at(base, k), :] for q in range(6)]
            damp = coef[7, at(base, k), :]
            pressure = []
            for w in range(2):
                exx = state[PARTS + 4 * w, at(base, k + 1), :] - state[PARTS + 4 * w, at(base, k), :]
                ezz = state[PARTS + 4 * w + 1, at(base, k + 1), :] + state[PARTS + 4 * w + 1, at(base, k), :]
                gxz = state[PARTS + 4 * w + 3, at(base, k + 1), :] + state[PARTS + 4 * w + 2, at(base, k), :]
                txx = c[0] * exx + c[1] * ezz + c[2] * gxz
                tzz = c[1] * exx + c[3] * ezz + c[4] * gxz
                txz = c[2] * exx + c[4] * ezz + c[5] * gxz
                sxx, szz, sxz = stress_at(w, base, k)
                if w == 0:
                    new = (sxx - txx, szz - tzz, sxz - txz)
                else:
                    new = (sxx + txx, szz + tzz, sxz + txz)
                new = tuple(v * damp for v in new)
                for q in range(3):
                    state[5 * w + 2 + q, at(base, k), :] = new[q]
                pressure.append(new[0] + new[1])
            image[at(base, k), :] += pressure[0] * pressure[1]

    def one_step(step, _):
        start = pl.multiple_of((step + PAD) * ROWS, ROWS)
        gradients(start, (0, 1))

        def turn(j, _):
            a = step + 2 * j
            base = pl.multiple_of((a + PAD) * ROWS, ROWS)
            velocities(a, base, (0, 1), step)
            gradients(base, (2, 3))
            stresses(base, (-3, -2))
            return 0

        lax.fori_loop(0, PHASE + 6 - step, turn, 0)
        return 0

    lax.fori_loop(1, PHASE + 1, one_step, 0)


def window(part):
    return pl.ds((PAD + part * COLS) * ROWS, COLS * ROWS)


def waves_kernel(waves_ref, out_ref):
    for tile in range(TILES):
        rows = pl.ds(row_of(tile), COLS, stride=ROWS)
        for q in range(10):
            out_ref[q, rows, :] = waves_ref[q, :, pl.ds(tile * 128, 128)]


def fetch(slabs, state, sems):
    copies = [
        pltpu.make_async_copy(ref, state.at[pl.ds(0, 10), window(part), :], sems.at[part])
        for part, ref in enumerate(slabs)
    ]
    for copy in copies:
        copy.start()
    return copies


def inject_kernel(traces_ref, tile_ref, col_ref, out_ref):
    cell = tile_ref[...] * COLS + col_ref[...]
    lane = lax.broadcasted_iota(jnp.int32, (128, 128), 0)
    out_ref[...] = lax.dot_general(
        traces_ref[...],
        jnp.where(cell + 2 * COLS == lane, 1.0, 0.0),
        (((1,), (1,)), ((), ())),
        precision=lax.Precision.HIGHEST,
        preferred_element_type=jnp.float32,
    )


def first_kernel(
    slabs,
    slab_ref,
    inject_ref,
    left_ref,
    own_ref,
    right_ref,
    coef_left_ref,
    coef_own_ref,
    coef_right_ref,
    state_out,
    coef,
    image_out,
    state,
    image,
    sems,
):
    copies = fetch((left_ref, own_ref, right_ref), state, sems)
    for part, store in enumerate((coef_left_ref, coef_own_ref, coef_right_ref)):
        base = (PAD + part * COLS) * ROWS
        for tile in range(TILES):
            rows = pl.ds(base + row_of(tile), COLS, stride=ROWS)
            for q in range(7):
                coef[q, rows, :] = 0.5 * store[tile, q].astype(jnp.float32)

    row = lax.broadcasted_iota(jnp.int32, (ROWS, 128), 0)
    z = (row % 8) * 512 + (row // 8) * 128 + lane_index()
    depth = ROWS * 128
    wide_z = jnp.maximum(jnp.maximum(PML - z, z - (depth - 1 - PML)), 0).astype(jnp.float32) / PML
    square_z = wide_z * wide_z
    slab = slab_ref[0]
    first = (slab - 1) * COLS

    def profile(i, _):
        x = first + i
        last = slabs * COLS - 1 - PML
        wide_x = jnp.maximum(jnp.maximum(PML - x, x - last), 0).astype(jnp.float32) * (1.0 / PML)
        rows = pl.ds(pl.multiple_of((i + PAD) * ROWS, ROWS), ROWS)
        coef[7, rows, :] = 1.0 - damping_peak * (wide_x * wide_x + square_z)
        return 0

    lax.fori_loop(0, WIDE, profile, 0)
    image[...] = jnp.zeros_like(image)
    for copy in copies:
        copy.wait()
    advance(state, coef, image, slab, inject_ref, 0)
    for q in range(10):
        state_out[q] = state[q, window(1), :]
    image_out[...] = image[window(1), :]


def second_kernel(
    slab_ref,
    inject_ref,
    left_ref,
    own_ref,
    right_ref,
    coef,
    image_in,
    waves_out,
    image_out,
    state,
    image,
    sems,
):
    copies = fetch((left_ref, own_ref, right_ref), state, sems)
    image[...] = jnp.zeros_like(image)
    image[window(1), :] = image_in[...]
    for copy in copies:
        copy.wait()
    advance(state, coef, image, slab_ref[0], inject_ref, PHASE)
    for tile in range(TILES):
        rows = pl.ds((PAD + COLS) * ROWS + row_of(tile), COLS, stride=ROWS)
        for q in range(10):
            waves_out[q, :, pl.ds(tile * 128, 128)] = state[q, rows, :]
        image_out[tile] = image[rows, :] * (1.0 / STEPS)


def stack_kernel(offsets_ref, pieces_ref, out_ref):
    out_ref[...] = jnp.zeros_like(out_ref)

    def one(shot, _):
        out_ref[offsets_ref[shot]] += pieces_ref[shot]
        return 0

    lax.fori_loop(0, pieces_ref.shape[0], one, 0)


VMEM = pl.BlockSpec(memory_space=pltpu.VMEM)
ANY = pl.BlockSpec(memory_space=pl.ANY)
SMEM = pl.BlockSpec(memory_space=pltpu.SMEM)
PARAMS = pltpu.CompilerParams(vmem_limit_bytes=VMEM_LIMIT)
LARGE = pltpu.CompilerParams(vmem_limit_bytes=56 * 1024 * 1024)


def shape(*dims, dtype=jnp.float32):
    return jax.ShapeDtypeStruct(dims, dtype)


def neighbours(block, axis):
    count = lax.axis_size(axis)
    up = [(i, i + 1) for i in range(count - 1)]
    down = [(i + 1, i) for i in range(count - 1)]
    return lax.ppermute(block, axis, up), lax.ppermute(block, axis, down)


def scratch():
    held = HELD * ROWS
    return [
        pltpu.VMEM((PLANES, held, 128), jnp.float32),
        pltpu.VMEM((held, 128), jnp.float32),
        pltpu.SemaphoreType.DMA((3,)),
    ]


def local(waves, traces, rec_tile, rec_col, offsets, directory, model_store):
    slabs = lax.axis_size("slab")
    shots = lax.axis_size("shot")
    depth = waves.shape[4]
    own = waves.reshape(10, COLS, depth)
    own_rows = COLS * ROWS

    def added(rows, bit):
        partner = [(i, i ^ bit) for i in range(slabs)]
        return rows + lax.ppermute(rows, "slab", partner)

    picked = pl.pallas_call(
        pick_kernel,
        out_shape=shape(shots, 7, COLS, 128, dtype=jnp.bfloat16),
        in_specs=[SMEM, SMEM, VMEM],
        out_specs=VMEM,
        compiler_params=LARGE,
    )(offsets, directory, model_store)
    picked, own, traces = lax.optimization_barrier((picked, own, traces))
    coef_own = lax.all_to_all(picked, "shot", split_axis=0, concat_axis=0, tiled=True)
    own = pl.pallas_call(
        waves_kernel,
        out_shape=shape(10, own_rows, 128),
        in_specs=[VMEM],
        out_specs=VMEM,
        compiler_params=PARAMS,
    )(own)
    left, right = neighbours(own, "slab")
    inject = pl.pallas_call(
        inject_kernel,
        out_shape=shape(STEPS, 128),
        in_specs=[VMEM] * 3,
        out_specs=VMEM,
        compiler_params=LARGE,
    )(traces[0], rec_tile.reshape(1, -1), rec_col)
    coef_own, inject = lax.optimization_barrier((coef_own, added(inject, 1)))
    inject = added(added(inject, 2), 4)
    slab = lax.axis_index("slab").astype(jnp.int32).reshape(1)
    coef_left, coef_right = neighbours(coef_own, "slab")
    state, coef, image = pl.pallas_call(
        functools.partial(first_kernel, slabs),
        out_shape=(shape(10, own_rows, 128), shape(8, HELD * ROWS, 128), shape(own_rows, 128)),
        in_specs=[SMEM, SMEM] + [ANY] * 3 + [VMEM] * 3,
        out_specs=(VMEM,) * 3,
        scratch_shapes=scratch(),
        compiler_params=PARAMS,
    )(slab, inject, left, own, right, coef_left, coef_own, coef_right)
    state_left, state_right = neighbours(state, "slab")
    waves_out, pieces = pl.pallas_call(
        second_kernel,
        out_shape=(shape(10, COLS, depth), shape(TILES, COLS, 128)),
        in_specs=[SMEM, SMEM] + [ANY] * 3 + [VMEM] * 2,
        out_specs=(VMEM,) * 2,
        scratch_shapes=scratch(),
        compiler_params=PARAMS,
    )(slab, inject, state_left, state, state_right, coef, image)
    pieces = lax.all_to_all(pieces, "shot", split_axis=0, concat_axis=0, tiled=True)
    stacked = pl.pallas_call(
        stack_kernel,
        out_shape=shape(model_store.shape[1], COLS, 128),
        in_specs=[SMEM, VMEM],
        out_specs=VMEM,
        compiler_params=PARAMS,
    )(offsets, pieces)
    return waves_out.reshape(waves.shape), stacked


def solution(mesh):
    placed = (
        P("shot", None, None, "slab", None),
        P("shot", None, "slab"),
        P("shot", "slab", None),
        P("shot", "slab"),
        P(),
        P(),
        P(None, None, "slab", "shot"),
    )
    return jax.shard_map(
        local,
        mesh=mesh,
        in_specs=placed,
        out_specs=(P("shot", None, None, "slab", None), P(None, "slab", "shot")),
        check_vma=False,
    )
```

```python
import functools

import jax
import jax.numpy as jnp
from jax import lax
from jax.experimental import pallas as pl
from jax.experimental.pallas import tpu as pltpu
from jax.sharding import PartitionSpec as P

STEPS = 16
PML = 16
REC_DEPTH = 24
damping_peak = 0.2

COLS = 8
TILES = 32
WIDE = 3 * COLS
PHASE = 8
PAD = 4
HELD = 36
GRADS, PARTS, PLANES = 10, 14, 22
ROWS = 32
VMEM_LIMIT = 32 * 1024 * 1024


def pick_kernel(offsets_ref, directory_ref, store_ref, out_ref):
    shots = out_ref.shape[0]

    def one(shot, _):
        slot = directory_ref[offsets_ref[shot]]
        for entry in range(7):
            out_ref[shot, entry] = store_ref[entry, slot]
        return 0

    lax.fori_loop(0, shots, one, 0)


def row_of(tile):
    return (tile % 4) * 8 + tile // 4


def iota8(axis):
    return lax.broadcasted_iota(jnp.int32, (8, 128), axis)


def lane_index():
    return lax.broadcasted_iota(jnp.int32, (ROWS, 128), 1)


def from_below(v, lane, sub):
    r = pltpu.roll(v, 1, 1)
    wrap = jnp.where(sub == 0, 0.0, pltpu.roll(r[24:32], 1, 0))
    return jnp.where(lane == 0, jnp.concatenate([wrap, r[0:24]], axis=0), r)


def from_above(v, lane, sub):
    r = pltpu.roll(v, 127, 1)
    wrap = jnp.where(sub == 7, 0.0, pltpu.roll(r[0:8], 7, 0))
    return jnp.where(lane == 127, jnp.concatenate([r[8:32], wrap], axis=0), r)


def advance(state, coef, image, slab, inject_ref, first_step):
    lane = lane_index()
    sub = iota8(0)
    spot = jnp.where((iota8(0) == 0) & (iota8(1) == REC_DEPTH), 1.0, 0.0)

    def at(base, k):
        return pl.ds(pl.multiple_of(base + k * ROWS, ROWS), ROWS)

    def stress_at(w, base, k):
        return tuple(state[5 * w + q, at(base, k), :] for q in (2, 3, 4))

    def gradients(base, ks):
        for w in range(2):
            left = stress_at(w, base, ks[0] - 1)
            for k in ks:
                here = stress_at(w, base, k)
                d, s = here[0] - left[0], here[2] + left[2]
                state[GRADS + 2 * w, at(base, k), :] = d + s + from_below(d - s, lane, sub)
                d, s = here[2] - left[2], here[1] + left[1]
                state[GRADS + 2 * w + 1, at(base, k), :] = d + s + from_below(d - s, lane, sub)
                left = here

    def velocities(a, base, ks, step):
        for k in ks:
            half_b = coef[6, at(base, k), :]
            damp = coef[7, at(base, k), :]
            for w in range(2):
                gx = half_b * state[GRADS + 2 * w, at(base, k), :]
                gz = half_b * state[GRADS + 2 * w + 1, at(base, k), :]
                vx = state[5 * w, at(base, k), :]
                vz = state[5 * w + 1, at(base, k), :]
                if w == 0:
                    vx, vz = vx - gx, vz - gz
                else:
                    vx, vz = vx + gx, vz + gz
                    add = inject_ref[first_step + step - 1, (slab + 1) * COLS + a + k]
                    vz = jnp.concatenate([vz[0:8] + add * spot, vz[8:32]], axis=0)
                state[5 * w, at(base, k), :] = vx * damp
                state[5 * w + 1, at(base, k), :] = vz * damp
                vx_z = from_above(vx, lane, sub)
                vz_z = from_above(vz, lane, sub)
                mx, pz = vx_z - vx, vz + vz_z
                state[PARTS + 4 * w, at(base, k), :] = vx + vx_z
                state[PARTS + 4 * w + 1, at(base, k), :] = vz_z - vz
                state[PARTS + 4 * w + 2, at(base, k), :] = mx - pz
                state[PARTS + 4 * w + 3, at(base, k), :] = mx + pz

    def stresses(base, ks):
        for k in ks:
            c = [coef[q, at(base, k), :] for q in range(6)]
            damp = coef[7, at(base, k), :]
            pressure = []
            for w in range(2):
                exx = state[PARTS + 4 * w, at(base, k + 1), :] - state[PARTS + 4 * w, at(base, k), :]
                ezz = state[PARTS + 4 * w + 1, at(base, k + 1), :] + state[PARTS + 4 * w + 1, at(base, k), :]
                gxz = state[PARTS + 4 * w + 3, at(base, k + 1), :] + state[PARTS + 4 * w + 2, at(base, k), :]
                txx = c[0] * exx + c[1] * ezz + c[2] * gxz
                tzz = c[1] * exx + c[3] * ezz + c[4] * gxz
                txz = c[2] * exx + c[4] * ezz + c[5] * gxz
                sxx, szz, sxz = stress_at(w, base, k)
                if w == 0:
                    new = (sxx - txx, szz - tzz, sxz - txz)
                else:
                    new = (sxx + txx, szz + tzz, sxz + txz)
                new = tuple(v * damp for v in new)
                for q in range(3):
                    state[5 * w + 2 + q, at(base, k), :] = new[q]
                pressure.append(new[0] + new[1])
            image[at(base, k), :] += pressure[0] * pressure[1]

    def base_of(a):
        return pl.multiple_of((a + PAD) * ROWS, ROWS)

    def one_step(step, _):
        start = base_of(step)
        gradients(start, (0, 1))
        velocities(step, start, (0, 1), step)
        gradients(start, (2, 3))

        def turn(j, _):
            a = step + 2 * j
            base = base_of(a)
            velocities(a, base, (0, 1), step)
            gradients(base, (2, 3))
            stresses(base, (-3, -2))
            return 0

        lax.fori_loop(1, PHASE + 5 - step, turn, 0)
        stresses(base_of(WIDE + 2 - step), (-3,))
        return 0

    lax.fori_loop(1, PHASE + 1, one_step, 0)


def window(part):
    return pl.ds((PAD + part * COLS) * ROWS, COLS * ROWS)


def waves_kernel(waves_ref, out_ref):
    for tile in range(TILES):
        rows = pl.ds(row_of(tile), COLS, stride=ROWS)
        for q in range(10):
            out_ref[q, rows, :] = waves_ref[q, :, pl.ds(tile * 128, 128)]


def fetch(slabs, state, sems):
    copies = [
        pltpu.make_async_copy(ref, state.at[pl.ds(0, 10), window(part), :], sems.at[part])
        for part, ref in enumerate(slabs)
    ]
    for copy in copies:
        copy.start()
    return copies


def inject_kernel(traces_ref, tile_ref, col_ref, out_ref):
    cell = tile_ref[...] * COLS + col_ref[...]
    lane = lax.broadcasted_iota(jnp.int32, (128, 128), 0)
    out_ref[...] = lax.dot_general(
        traces_ref[...],
        jnp.where(cell + 2 * COLS == lane, 1.0, 0.0),
        (((1,), (1,)), ((), ())),
        precision=lax.Precision.HIGHEST,
        preferred_element_type=jnp.float32,
    )


def first_kernel(
    slabs,
    slab_ref,
    inject_ref,
    left_ref,
    own_ref,
    right_ref,
    coef_left_ref,
    coef_own_ref,
    coef_right_ref,
    state_out,
    coef,
    image_out,
    state,
    image,
    sems,
):
    copies = fetch((left_ref, own_ref, right_ref), state, sems)
    for part, store in enumerate((coef_left_ref, coef_own_ref, coef_right_ref)):
        base = (PAD + part * COLS) * ROWS
        for tile in range(TILES):
            rows = pl.ds(base + row_of(tile), COLS, stride=ROWS)
            for q in range(7):
                coef[q, rows, :] = 0.5 * store[tile, q].astype(jnp.float32)

    row = lax.broadcasted_iota(jnp.int32, (ROWS, 128), 0)
    z = (row % 8) * 512 + (row // 8) * 128 + lane_index()
    depth = ROWS * 128
    wide_z = jnp.maximum(jnp.maximum(PML - z, z - (depth - 1 - PML)), 0).astype(jnp.float32) / PML
    square_z = wide_z * wide_z
    slab = slab_ref[0]
    first = (slab - 1) * COLS

    def profile(i, _):
        x = first + i
        last = slabs * COLS - 1 - PML
        wide_x = jnp.maximum(jnp.maximum(PML - x, x - last), 0).astype(jnp.float32) * (1.0 / PML)
        rows = pl.ds(pl.multiple_of((i + PAD) * ROWS, ROWS), ROWS)
        coef[7, rows, :] = 1.0 - damping_peak * (wide_x * wide_x + square_z)
        return 0

    lax.fori_loop(0, WIDE, profile, 0)
    image[...] = jnp.zeros_like(image)
    for copy in copies:
        copy.wait()
    advance(state, coef, image, slab, inject_ref, 0)
    for q in range(10):
        state_out[q] = state[q, window(1), :]
    image_out[...] = image[window(1), :]


def second_kernel(
    slab_ref,
    inject_ref,
    left_ref,
    own_ref,
    right_ref,
    coef,
    image_in,
    state_out,
    image_out,
    state,
    image,
    sems,
):
    copies = fetch((left_ref, own_ref, right_ref), state, sems)
    image[...] = jnp.zeros_like(image)
    image[window(1), :] = image_in[...]
    for copy in copies:
        copy.wait()
    advance(state, coef, image, slab_ref[0], inject_ref, PHASE)
    for q in range(10):
        state_out[q] = state[q, window(1), :]
    for tile in range(TILES):
        rows = pl.ds((PAD + COLS) * ROWS + row_of(tile), COLS, stride=ROWS)
        image_out[tile] = image[rows, :] * (1.0 / STEPS)


def final_kernel(state_ref, waves_out):
    for tile in range(TILES):
        rows = pl.ds(row_of(tile), COLS, stride=ROWS)
        for q in range(10):
            waves_out[q, :, pl.ds(tile * 128, 128)] = state_ref[q, rows, :]


def stack_kernel(offsets_ref, pieces_ref, out_ref):
    out_ref[...] = jnp.zeros_like(out_ref)

    def one(shot, _):
        out_ref[offsets_ref[shot]] += pieces_ref[shot]
        return 0

    lax.fori_loop(0, pieces_ref.shape[0], one, 0)


VMEM = pl.BlockSpec(memory_space=pltpu.VMEM)
ANY = pl.BlockSpec(memory_space=pl.ANY)
SMEM = pl.BlockSpec(memory_space=pltpu.SMEM)
PARAMS = pltpu.CompilerParams(vmem_limit_bytes=VMEM_LIMIT)
LARGE = pltpu.CompilerParams(vmem_limit_bytes=56 * 1024 * 1024)


def shape(*dims, dtype=jnp.float32):
    return jax.ShapeDtypeStruct(dims, dtype)


def neighbours(block, axis):
    count = lax.axis_size(axis)
    up = [(i, i + 1) for i in range(count - 1)]
    down = [(i + 1, i) for i in range(count - 1)]
    return lax.ppermute(block, axis, up), lax.ppermute(block, axis, down)


def scratch():
    held = HELD * ROWS
    return [
        pltpu.VMEM((PLANES, held, 128), jnp.float32),
        pltpu.VMEM((held, 128), jnp.float32),
        pltpu.SemaphoreType.DMA((3,)),
    ]


def local(waves, traces, rec_tile, rec_col, offsets, directory, model_store):
    slabs = lax.axis_size("slab")
    shots = lax.axis_size("shot")
    depth = waves.shape[4]
    own = waves.reshape(10, COLS, depth)
    own_rows = COLS * ROWS

    def exchanged(rows, bits):
        return lax.ppermute(rows, "slab", [(i, i ^ bits) for i in range(slabs)])

    picked = pl.pallas_call(
        pick_kernel,
        out_shape=shape(shots, 7, COLS, 128, dtype=jnp.bfloat16),
        in_specs=[SMEM, SMEM, VMEM],
        out_specs=VMEM,
        compiler_params=LARGE,
    )(offsets, directory, model_store)
    picked, own, traces = lax.optimization_barrier((picked, own, traces))
    coef_own = lax.all_to_all(picked, "shot", split_axis=0, concat_axis=0, tiled=True)
    own = pl.pallas_call(
        waves_kernel,
        out_shape=shape(10, own_rows, 128),
        in_specs=[VMEM],
        out_specs=VMEM,
        compiler_params=PARAMS,
    )(own)
    left, right = neighbours(own, "slab")
    inject = pl.pallas_call(
        inject_kernel,
        out_shape=shape(STEPS, 128),
        in_specs=[VMEM] * 3,
        out_specs=VMEM,
        compiler_params=LARGE,
    )(traces[0], rec_tile.reshape(1, -1), rec_col)
    coef_own, inject = lax.optimization_barrier((coef_own, inject + exchanged(inject, 1)))
    left, right, inject = lax.optimization_barrier((left, right, inject))
    inject = inject + sum(exchanged(inject, bits) for bits in range(2, slabs, 2))
    slab = lax.axis_index("slab").astype(jnp.int32).reshape(1)
    coef_left, coef_right = neighbours(coef_own, "slab")
    state, coef, image = pl.pallas_call(
        functools.partial(first_kernel, slabs),
        out_shape=(shape(10, own_rows, 128), shape(8, HELD * ROWS, 128), shape(own_rows, 128)),
        in_specs=[SMEM, SMEM] + [ANY] * 3 + [VMEM] * 3,
        out_specs=(VMEM,) * 3,
        scratch_shapes=scratch(),
        compiler_params=PARAMS,
    )(slab, inject, left, own, right, coef_left, coef_own, coef_right)
    state_left, state_right = neighbours(state, "slab")
    state, pieces = pl.pallas_call(
        second_kernel,
        out_shape=(shape(10, own_rows, 128), shape(TILES, COLS, 128)),
        in_specs=[SMEM, SMEM] + [ANY] * 3 + [VMEM] * 2,
        out_specs=(VMEM,) * 2,
        scratch_shapes=scratch(),
        compiler_params=PARAMS,
    )(slab, inject, state_left, state, state_right, coef, image)
    pieces = lax.all_to_all(pieces, "shot", split_axis=0, concat_axis=0, tiled=True)
    waves_out = pl.pallas_call(
        final_kernel,
        out_shape=shape(10, COLS, depth),
        in_specs=[VMEM],
        out_specs=VMEM,
        compiler_params=PARAMS,
    )(state)
    stacked = pl.pallas_call(
        stack_kernel,
        out_shape=shape(model_store.shape[1], COLS, 128),
        in_specs=[SMEM, VMEM],
        out_specs=VMEM,
        compiler_params=PARAMS,
    )(offsets, pieces)
    return waves_out.reshape(waves.shape), stacked


def solution(mesh):
    placed = (
        P("shot", None, None, "slab", None),
        P("shot", None, "slab"),
        P("shot", "slab", None),
        P("shot", "slab"),
        P(),
        P(),
        P(None, None, "slab", "shot"),
    )
    return jax.shard_map(
        local,
        mesh=mesh,
        in_specs=placed,
        out_specs=(P("shot", None, None, "slab", None), P(None, "slab", "shot")),
        check_vma=False,
    )
```

```python
import functools

import jax
import jax.numpy as jnp
from jax import lax
from jax.experimental import pallas as pl
from jax.experimental.pallas import tpu as pltpu
from jax.sharding import PartitionSpec as P

STEPS = 16
PML = 16
REC_DEPTH = 24
damping_peak = 0.2

COLS = 8
TILES = 32
WIDE = 3 * COLS
PHASE = 8
PAD = 4
HELD = 36
GRADS, PARTS, PLANES = 10, 14, 22
ROWS = 32
VMEM_LIMIT = 32 * 1024 * 1024


def pick_kernel(offsets_ref, directory_ref, store_ref, out_ref):
    shots = out_ref.shape[0]

    def one(shot, _):
        slot = directory_ref[offsets_ref[shot]]
        for entry in range(7):
            out_ref[shot, entry] = store_ref[entry, slot]
        return 0

    lax.fori_loop(0, shots, one, 0)


def row_of(tile):
    return (tile % 4) * 8 + tile // 4


def iota8(axis):
    return lax.broadcasted_iota(jnp.int32, (8, 128), axis)


def lane_index():
    return lax.broadcasted_iota(jnp.int32, (ROWS, 128), 1)


def from_below(v, lane, sub):
    r = pltpu.roll(v, 1, 1)
    wrap = jnp.where(sub == 0, 0.0, pltpu.roll(r[24:32], 1, 0))
    return jnp.where(lane == 0, jnp.concatenate([wrap, r[0:24]], axis=0), r)


def from_above(v, lane, sub):
    r = pltpu.roll(v, 127, 1)
    wrap = jnp.where(sub == 7, 0.0, pltpu.roll(r[0:8], 7, 0))
    return jnp.where(lane == 127, jnp.concatenate([r[8:32], wrap], axis=0), r)


def advance(state, coef, image, slab, inject_ref, first_step):
    lane = lane_index()
    sub = iota8(0)
    spot = jnp.where((iota8(0) == 0) & (iota8(1) == REC_DEPTH), 1.0, 0.0)

    def at(base, k):
        return pl.ds(pl.multiple_of(base + k * ROWS, ROWS), ROWS)

    def stress_at(w, base, k):
        return tuple(state[5 * w + q, at(base, k), :] for q in (2, 3, 4))

    def gradients(base, ks):
        for w in range(2):
            left = stress_at(w, base, ks[0] - 1)
            for k in ks:
                here = stress_at(w, base, k)
                d, s = here[0] - left[0], here[2] + left[2]
                state[GRADS + 2 * w, at(base, k), :] = d + s + from_below(d - s, lane, sub)
                d, s = here[2] - left[2], here[1] + left[1]
                state[GRADS + 2 * w + 1, at(base, k), :] = d + s + from_below(d - s, lane, sub)
                left = here

    def velocities(a, base, ks, step):
        for k in ks:
            half_b = coef[6, at(base, k), :]
            damp = coef[7, at(base, k), :]
            for w in range(2):
                gx = half_b * state[GRADS + 2 * w, at(base, k), :]
                gz = half_b * state[GRADS + 2 * w + 1, at(base, k), :]
                vx = state[5 * w, at(base, k), :]
                vz = state[5 * w + 1, at(base, k), :]
                if w == 0:
                    vx, vz = vx - gx, vz - gz
                else:
                    vx, vz = vx + gx, vz + gz
                    add = inject_ref[first_step + step - 1, (slab + 1) * COLS + a + k]
                    vz = jnp.concatenate([vz[0:8] + add * spot, vz[8:32]], axis=0)
                state[5 * w, at(base, k), :] = vx * damp
                state[5 * w + 1, at(base, k), :] = vz * damp
                vx_z = from_above(vx, lane, sub)
                vz_z = from_above(vz, lane, sub)
                mx, pz = vx_z - vx, vz + vz_z
                state[PARTS + 4 * w, at(base, k), :] = vx + vx_z
                state[PARTS + 4 * w + 1, at(base, k), :] = vz_z - vz
                state[PARTS + 4 * w + 2, at(base, k), :] = mx - pz
                state[PARTS + 4 * w + 3, at(base, k), :] = mx + pz

    def stresses(base, ks):
        for k in ks:
            c = [coef[q, at(base, k), :] for q in range(6)]
            damp = coef[7, at(base, k), :]
            pressure = []
            for w in range(2):
                exx = state[PARTS + 4 * w, at(base, k + 1), :] - state[PARTS + 4 * w, at(base, k), :]
                ezz = state[PARTS + 4 * w + 1, at(base, k + 1), :] + state[PARTS + 4 * w + 1, at(base, k), :]
                gxz = state[PARTS + 4 * w + 3, at(base, k + 1), :] + state[PARTS + 4 * w + 2, at(base, k), :]
                txx = c[0] * exx + c[1] * ezz + c[2] * gxz
                tzz = c[1] * exx + c[3] * ezz + c[4] * gxz
                txz = c[2] * exx + c[4] * ezz + c[5] * gxz
                sxx, szz, sxz = stress_at(w, base, k)
                if w == 0:
                    new = (sxx - txx, szz - tzz, sxz - txz)
                else:
                    new = (sxx + txx, szz + tzz, sxz + txz)
                new = tuple(v * damp for v in new)
                for q in range(3):
                    state[5 * w + 2 + q, at(base, k), :] = new[q]
                pressure.append(new[0] + new[1])
            image[at(base, k), :] += pressure[0] * pressure[1]

    def base_of(a):
        return pl.multiple_of((a + PAD) * ROWS, ROWS)

    def one_step(step, _):
        start = base_of(step)
        gradients(start, (0, 1))
        velocities(step, start, (0, 1), step)
        gradients(start, (2, 3))

        def turn(j, _):
            a = step + 2 * j
            base = base_of(a)
            velocities(a, base, (0, 1), step)
            gradients(base, (2, 3))
            stresses(base, (-3, -2))
            return 0

        lax.fori_loop(1, PHASE + 5 - step, turn, 0)
        stresses(base_of(WIDE + 2 - step), (-3,))
        return 0

    lax.fori_loop(1, PHASE + 1, one_step, 0)


def window(part):
    return pl.ds((PAD + part * COLS) * ROWS, COLS * ROWS)


def waves_kernel(waves_ref, out_ref):
    for tile in range(TILES):
        rows = pl.ds(row_of(tile), COLS, stride=ROWS)
        for q in range(10):
            out_ref[q, rows, :] = waves_ref[q, :, pl.ds(tile * 128, 128)]


def fetch(slabs, state, sems):
    copies = [
        pltpu.make_async_copy(ref, state.at[pl.ds(0, 10), window(part), :], sems.at[part])
        for part, ref in enumerate(slabs)
    ]
    for copy in copies:
        copy.start()
    return copies


def inject_kernel(traces_ref, tile_ref, col_ref, out_ref):
    cell = tile_ref[...] * COLS + col_ref[...]
    lane = lax.broadcasted_iota(jnp.int32, (128, 128), 0)
    out_ref[...] = lax.dot_general(
        traces_ref[...],
        jnp.where(cell + 2 * COLS == lane, 1.0, 0.0),
        (((1,), (1,)), ((), ())),
        precision=lax.Precision.HIGHEST,
        preferred_element_type=jnp.float32,
    )


def first_kernel(
    slabs,
    slab_ref,
    inject_ref,
    left_ref,
    own_ref,
    right_ref,
    coef_left_ref,
    coef_own_ref,
    coef_right_ref,
    state_out,
    coef,
    image_out,
    state,
    image,
    sems,
):
    copies = fetch((left_ref, own_ref, right_ref), state, sems)
    for part, store in enumerate((coef_left_ref, coef_own_ref, coef_right_ref)):
        base = (PAD + part * COLS) * ROWS
        for tile in range(TILES):
            rows = pl.ds(base + row_of(tile), COLS, stride=ROWS)
            for q in range(7):
                coef[q, rows, :] = 0.5 * store[tile, q].astype(jnp.float32)

    row = lax.broadcasted_iota(jnp.int32, (ROWS, 128), 0)
    z = (row % 8) * 512 + (row // 8) * 128 + lane_index()
    depth = ROWS * 128
    wide_z = jnp.maximum(jnp.maximum(PML - z, z - (depth - 1 - PML)), 0).astype(jnp.float32) / PML
    square_z = wide_z * wide_z
    slab = slab_ref[0]
    first = (slab - 1) * COLS

    def profile(i, _):
        x = first + i
        last = slabs * COLS - 1 - PML
        wide_x = jnp.maximum(jnp.maximum(PML - x, x - last), 0).astype(jnp.float32) * (1.0 / PML)
        rows = pl.ds(pl.multiple_of((i + PAD) * ROWS, ROWS), ROWS)
        coef[7, rows, :] = 1.0 - damping_peak * (wide_x * wide_x + square_z)
        return 0

    lax.fori_loop(0, WIDE, profile, 0)
    image[...] = jnp.zeros_like(image)
    for copy in copies:
        copy.wait()
    advance(state, coef, image, slab, inject_ref, 0)
    for q in range(10):
        state_out[q] = state[q, window(1), :]
    image_out[...] = image[window(1), :]


def second_kernel(
    slab_ref,
    inject_ref,
    left_ref,
    own_ref,
    right_ref,
    coef,
    image_in,
    state_out,
    image_out,
    state,
    image,
    sems,
):
    copies = fetch((left_ref, own_ref, right_ref), state, sems)
    image[...] = jnp.zeros_like(image)
    image[window(1), :] = image_in[...]
    for copy in copies:
        copy.wait()
    advance(state, coef, image, slab_ref[0], inject_ref, PHASE)
    for q in range(10):
        state_out[q] = state[q, window(1), :]
    for tile in range(TILES):
        rows = pl.ds((PAD + COLS) * ROWS + row_of(tile), COLS, stride=ROWS)
        image_out[tile] = image[rows, :] * (1.0 / STEPS)


def final_kernel(state_ref, waves_out):
    for tile in range(TILES):
        rows = pl.ds(row_of(tile), COLS, stride=ROWS)
        for q in range(10):
            waves_out[q, :, pl.ds(tile * 128, 128)] = state_ref[q, rows, :]


def stack_kernel(offsets_ref, pieces_ref, out_ref):
    out_ref[...] = jnp.zeros_like(out_ref)

    def one(shot, _):
        out_ref[offsets_ref[shot]] += pieces_ref[shot]
        return 0

    lax.fori_loop(0, pieces_ref.shape[0], one, 0)


VMEM = pl.BlockSpec(memory_space=pltpu.VMEM)
ANY = pl.BlockSpec(memory_space=pl.ANY)
SMEM = pl.BlockSpec(memory_space=pltpu.SMEM)
PARAMS = pltpu.CompilerParams(vmem_limit_bytes=VMEM_LIMIT)
LARGE = pltpu.CompilerParams(vmem_limit_bytes=56 * 1024 * 1024)


def shape(*dims, dtype=jnp.float32):
    return jax.ShapeDtypeStruct(dims, dtype)


def neighbours(block, axis):
    count = lax.axis_size(axis)
    up = [(i, i + 1) for i in range(count - 1)]
    down = [(i + 1, i) for i in range(count - 1)]
    return lax.ppermute(block, axis, up), lax.ppermute(block, axis, down)


def scratch():
    held = HELD * ROWS
    return [
        pltpu.VMEM((PLANES, held, 128), jnp.float32),
        pltpu.VMEM((held, 128), jnp.float32),
        pltpu.SemaphoreType.DMA((3,)),
    ]


def local(waves, traces, rec_tile, rec_col, offsets, directory, model_store):
    slabs = lax.axis_size("slab")
    shots = lax.axis_size("shot")
    depth = waves.shape[4]
    own = waves.reshape(10, COLS, depth)
    own_rows = COLS * ROWS

    def exchanged(rows, bits):
        return lax.ppermute(rows, "slab", [(i, i ^ bits) for i in range(slabs)])

    picked = pl.pallas_call(
        pick_kernel,
        out_shape=shape(shots, 7, COLS, 128, dtype=jnp.bfloat16),
        in_specs=[SMEM, SMEM, VMEM],
        out_specs=VMEM,
        compiler_params=LARGE,
    )(offsets, directory, model_store)
    picked, own, traces = lax.optimization_barrier((picked, own, traces))
    coef_own = lax.all_to_all(picked, "shot", split_axis=0, concat_axis=0, tiled=True)
    own = pl.pallas_call(
        waves_kernel,
        out_shape=shape(10, own_rows, 128),
        in_specs=[VMEM],
        out_specs=VMEM,
        compiler_params=PARAMS,
    )(own)
    left, right = neighbours(own, "slab")
    inject = pl.pallas_call(
        inject_kernel,
        out_shape=shape(STEPS, 128),
        in_specs=[VMEM] * 3,
        out_specs=VMEM,
        compiler_params=LARGE,
    )(traces[0], rec_tile.reshape(1, -1), rec_col)
    coef_own, inject = lax.optimization_barrier((coef_own, inject + exchanged(inject, 1)))
    bit = 2
    while bit < slabs:
        inject = inject + exchanged(inject, bit)
        bit *= 2
    slab = lax.axis_index("slab").astype(jnp.int32).reshape(1)
    coef_left, coef_right = neighbours(coef_own, "slab")
    state, coef, image = pl.pallas_call(
        functools.partial(first_kernel, slabs),
        out_shape=(shape(10, own_rows, 128), shape(8, HELD * ROWS, 128), shape(own_rows, 128)),
        in_specs=[SMEM, SMEM] + [ANY] * 3 + [VMEM] * 3,
        out_specs=(VMEM,) * 3,
        scratch_shapes=scratch(),
        compiler_params=PARAMS,
    )(slab, inject, left, own, right, coef_left, coef_own, coef_right)
    state_left, state_right = neighbours(state, "slab")
    state, pieces = pl.pallas_call(
        second_kernel,
        out_shape=(shape(10, own_rows, 128), shape(TILES, COLS, 128)),
        in_specs=[SMEM, SMEM] + [ANY] * 3 + [VMEM] * 2,
        out_specs=(VMEM,) * 2,
        scratch_shapes=scratch(),
        compiler_params=PARAMS,
    )(slab, inject, state_left, state, state_right, coef, image)
    pieces = lax.all_to_all(pieces, "shot", split_axis=0, concat_axis=0, tiled=True)
    waves_out = pl.pallas_call(
        final_kernel,
        out_shape=shape(10, COLS, depth),
        in_specs=[VMEM],
        out_specs=VMEM,
        compiler_params=PARAMS,
    )(state)
    stacked = pl.pallas_call(
        stack_kernel,
        out_shape=shape(model_store.shape[1], COLS, 128),
        in_specs=[SMEM, VMEM],
        out_specs=VMEM,
        compiler_params=PARAMS,
    )(offsets, pieces)
    return waves_out.reshape(waves.shape), stacked


def solution(mesh):
    placed = (
        P("shot", None, None, "slab", None),
        P("shot", None, "slab"),
        P("shot", "slab", None),
        P("shot", "slab"),
        P(),
        P(),
        P(None, None, "slab", "shot"),
    )
    return jax.shard_map(
        local,
        mesh=mesh,
        in_specs=placed,
        out_specs=(P("shot", None, None, "slab", None), P(None, "slab", "shot")),
        check_vma=False,
    )
```

```python
import functools

import jax
import jax.numpy as jnp
from jax import lax
from jax.experimental import pallas as pl
from jax.experimental.pallas import tpu as pltpu
from jax.sharding import PartitionSpec as P

STEPS = 16
PML = 16
REC_DEPTH = 24
damping_peak = 0.2

COLS = 8
TILES = 32
WIDE = 3 * COLS
PHASE = 8
PAD = 4
HELD = 36
GRADS, PARTS, PLANES = 10, 14, 22
ROWS = 32
VMEM_LIMIT = 32 * 1024 * 1024


def pick_kernel(offsets_ref, directory_ref, store_ref, out_ref):
    shots = out_ref.shape[0]

    def one(shot, _):
        slot = directory_ref[offsets_ref[shot]]
        for entry in range(7):
            out_ref[shot, entry] = store_ref[entry, slot]
        return 0

    lax.fori_loop(0, shots, one, 0)


def row_of(tile):
    return (tile % 4) * 8 + tile // 4


def iota8(axis):
    return lax.broadcasted_iota(jnp.int32, (8, 128), axis)


def lane_index():
    return lax.broadcasted_iota(jnp.int32, (ROWS, 128), 1)


def from_below(v, lane, sub):
    r = pltpu.roll(v, 1, 1)
    wrap = jnp.where(sub == 0, 0.0, pltpu.roll(r[24:32], 1, 0))
    return jnp.where(lane == 0, jnp.concatenate([wrap, r[0:24]], axis=0), r)


def from_above(v, lane, sub):
    r = pltpu.roll(v, 127, 1)
    wrap = jnp.where(sub == 7, 0.0, pltpu.roll(r[0:8], 7, 0))
    return jnp.where(lane == 127, jnp.concatenate([r[8:32], wrap], axis=0), r)


def advance(state, coef, image, slab, inject_ref, first_step):
    lane = lane_index()
    sub = iota8(0)
    spot = jnp.where((iota8(0) == 0) & (iota8(1) == REC_DEPTH), 1.0, 0.0)

    def at(base, k):
        return pl.ds(pl.multiple_of(base + k * ROWS, ROWS), ROWS)

    def stress_at(w, base, k):
        return tuple(state[5 * w + q, at(base, k), :] for q in (2, 3, 4))

    def gradients(base, ks):
        for w in range(2):
            left = stress_at(w, base, ks[0] - 1)
            for k in ks:
                here = stress_at(w, base, k)
                d, s = here[0] - left[0], here[2] + left[2]
                state[GRADS + 2 * w, at(base, k), :] = d + s + from_below(d - s, lane, sub)
                d, s = here[2] - left[2], here[1] + left[1]
                state[GRADS + 2 * w + 1, at(base, k), :] = d + s + from_below(d - s, lane, sub)
                left = here

    def velocities(a, base, ks, step):
        for k in ks:
            half_b = coef[6, at(base, k), :]
            damp = coef[7, at(base, k), :]
            for w in range(2):
                gx = half_b * state[GRADS + 2 * w, at(base, k), :]
                gz = half_b * state[GRADS + 2 * w + 1, at(base, k), :]
                vx = state[5 * w, at(base, k), :]
                vz = state[5 * w + 1, at(base, k), :]
                if w == 0:
                    vx, vz = vx - gx, vz - gz
                else:
                    vx, vz = vx + gx, vz + gz
                    add = inject_ref[first_step + step - 1, (slab + 1) * COLS + a + k]
                    vz = jnp.concatenate([vz[0:8] + add * spot, vz[8:32]], axis=0)
                state[5 * w, at(base, k), :] = vx * damp
                state[5 * w + 1, at(base, k), :] = vz * damp
                vx_z = from_above(vx, lane, sub)
                vz_z = from_above(vz, lane, sub)
                mx, pz = vx_z - vx, vz + vz_z
                state[PARTS + 4 * w, at(base, k), :] = vx + vx_z
                state[PARTS + 4 * w + 1, at(base, k), :] = vz_z - vz
                state[PARTS + 4 * w + 2, at(base, k), :] = mx - pz
                state[PARTS + 4 * w + 3, at(base, k), :] = mx + pz

    def stresses(base, ks):
        for k in ks:
            c = [coef[q, at(base, k), :] for q in range(6)]
            damp = coef[7, at(base, k), :]
            pressure = []
            for w in range(2):
                exx = state[PARTS + 4 * w, at(base, k + 1), :] - state[PARTS + 4 * w, at(base, k), :]
                ezz = state[PARTS + 4 * w + 1, at(base, k + 1), :] + state[PARTS + 4 * w + 1, at(base, k), :]
                gxz = state[PARTS + 4 * w + 3, at(base, k + 1), :] + state[PARTS + 4 * w + 2, at(base, k), :]
                txx = c[0] * exx + c[1] * ezz + c[2] * gxz
                tzz = c[1] * exx + c[3] * ezz + c[4] * gxz
                txz = c[2] * exx + c[4] * ezz + c[5] * gxz
                sxx, szz, sxz = stress_at(w, base, k)
                if w == 0:
                    new = (sxx - txx, szz - tzz, sxz - txz)
                else:
                    new = (sxx + txx, szz + tzz, sxz + txz)
                new = tuple(v * damp for v in new)
                for q in range(3):
                    state[5 * w + 2 + q, at(base, k), :] = new[q]
                pressure.append(new[0] + new[1])
            image[at(base, k), :] += pressure[0] * pressure[1]

    def base_of(a):
        return pl.multiple_of((a + PAD) * ROWS, ROWS)

    def one_step(step, _):
        start = base_of(step)
        gradients(start, (0, 1))
        velocities(step, start, (0, 1), step)
        gradients(start, (2, 3))

        def turn(j, _):
            a = step + 2 * j
            base = base_of(a)
            velocities(a, base, (0, 1), step)
            gradients(base, (2, 3))
            stresses(base, (-3, -2))
            return 0

        lax.fori_loop(1, PHASE + 5 - step, turn, 0)
        stresses(base_of(WIDE + 2 - step), (-3,))
        return 0

    lax.fori_loop(1, PHASE + 1, one_step, 0)


def window(part):
    return pl.ds((PAD + part * COLS) * ROWS, COLS * ROWS)


def waves_kernel(waves_ref, out_ref):
    for tile in range(TILES):
        rows = pl.ds(row_of(tile), COLS, stride=ROWS)
        for q in range(10):
            out_ref[q, rows, :] = waves_ref[q, :, pl.ds(tile * 128, 128)]


def fetch(slabs, state, sems):
    copies = [
        pltpu.make_async_copy(ref, state.at[pl.ds(0, 10), window(part), :], sems.at[part])
        for part, ref in enumerate(slabs)
    ]
    for copy in copies:
        copy.start()
    return copies


def inject_kernel(traces_ref, tile_ref, col_ref, out_ref):
    cell = tile_ref[...] * COLS + col_ref[...]
    lane = lax.broadcasted_iota(jnp.int32, (128, 128), 0)
    out_ref[...] = lax.dot_general(
        traces_ref[...],
        jnp.where(cell + 2 * COLS == lane, 1.0, 0.0),
        (((1,), (1,)), ((), ())),
        precision=lax.Precision.HIGHEST,
        preferred_element_type=jnp.float32,
    )


def coef_kernel(slabs, slab_ref, coef_left_ref, coef_own_ref, coef_right_ref, coef):
    for part, store in enumerate((coef_left_ref, coef_own_ref, coef_right_ref)):
        base = (PAD + part * COLS) * ROWS
        for tile in range(TILES):
            rows = pl.ds(base + row_of(tile), COLS, stride=ROWS)
            for q in range(7):
                coef[q, rows, :] = 0.5 * store[tile, q].astype(jnp.float32)

    row = lax.broadcasted_iota(jnp.int32, (ROWS, 128), 0)
    z = (row % 8) * 512 + (row // 8) * 128 + lane_index()
    depth = ROWS * 128
    wide_z = jnp.maximum(jnp.maximum(PML - z, z - (depth - 1 - PML)), 0).astype(jnp.float32) / PML
    square_z = wide_z * wide_z
    first = (slab_ref[0] - 1) * COLS

    def profile(i, _):
        x = first + i
        last = slabs * COLS - 1 - PML
        wide_x = jnp.maximum(jnp.maximum(PML - x, x - last), 0).astype(jnp.float32) * (1.0 / PML)
        rows = pl.ds(pl.multiple_of((i + PAD) * ROWS, ROWS), ROWS)
        coef[7, rows, :] = 1.0 - damping_peak * (wide_x * wide_x + square_z)
        return 0

    lax.fori_loop(0, WIDE, profile, 0)


def first_kernel(
    slab_ref,
    inject_ref,
    left_ref,
    own_ref,
    right_ref,
    coef,
    state_out,
    image_out,
    state,
    image,
    sems,
):
    copies = fetch((left_ref, own_ref, right_ref), state, sems)
    image[...] = jnp.zeros_like(image)
    for copy in copies:
        copy.wait()
    advance(state, coef, image, slab_ref[0], inject_ref, 0)
    for q in range(10):
        state_out[q] = state[q, window(1), :]
    image_out[...] = image[window(1), :]


def second_kernel(
    slab_ref,
    inject_ref,
    left_ref,
    own_ref,
    right_ref,
    coef,
    image_in,
    state_out,
    image_out,
    state,
    image,
    sems,
):
    copies = fetch((left_ref, own_ref, right_ref), state, sems)
    image[...] = jnp.zeros_like(image)
    image[window(1), :] = image_in[...]
    for copy in copies:
        copy.wait()
    advance(state, coef, image, slab_ref[0], inject_ref, PHASE)
    for q in range(10):
        state_out[q] = state[q, window(1), :]
    for tile in range(TILES):
        rows = pl.ds((PAD + COLS) * ROWS + row_of(tile), COLS, stride=ROWS)
        image_out[tile] = image[rows, :] * (1.0 / STEPS)


def final_kernel(state_ref, waves_out):
    for tile in range(TILES):
        rows = pl.ds(row_of(tile), COLS, stride=ROWS)
        for q in range(10):
            waves_out[q, :, pl.ds(tile * 128, 128)] = state_ref[q, rows, :]


def stack_kernel(offsets_ref, pieces_ref, out_ref):
    out_ref[...] = jnp.zeros_like(out_ref)

    def one(shot, _):
        out_ref[offsets_ref[shot]] += pieces_ref[shot]
        return 0

    lax.fori_loop(0, pieces_ref.shape[0], one, 0)


VMEM = pl.BlockSpec(memory_space=pltpu.VMEM)
ANY = pl.BlockSpec(memory_space=pl.ANY)
SMEM = pl.BlockSpec(memory_space=pltpu.SMEM)
PARAMS = pltpu.CompilerParams(vmem_limit_bytes=VMEM_LIMIT)
LARGE = pltpu.CompilerParams(vmem_limit_bytes=56 * 1024 * 1024)


def shape(*dims, dtype=jnp.float32):
    return jax.ShapeDtypeStruct(dims, dtype)


def neighbours(block, axis):
    count = lax.axis_size(axis)
    up = [(i, i + 1) for i in range(count - 1)]
    down = [(i + 1, i) for i in range(count - 1)]
    return lax.ppermute(block, axis, up), lax.ppermute(block, axis, down)


def scratch():
    held = HELD * ROWS
    return [
        pltpu.VMEM((PLANES, held, 128), jnp.float32),
        pltpu.VMEM((held, 128), jnp.float32),
        pltpu.SemaphoreType.DMA((3,)),
    ]


def local(waves, traces, rec_tile, rec_col, offsets, directory, model_store):
    slabs = lax.axis_size("slab")
    shots = lax.axis_size("shot")
    depth = waves.shape[4]
    own = waves.reshape(10, COLS, depth)
    own_rows = COLS * ROWS

    def exchanged(rows, bits):
        return lax.ppermute(rows, "slab", [(i, i ^ bits) for i in range(slabs)])

    picked = pl.pallas_call(
        pick_kernel,
        out_shape=shape(shots, 7, COLS, 128, dtype=jnp.bfloat16),
        in_specs=[SMEM, SMEM, VMEM],
        out_specs=VMEM,
        compiler_params=LARGE,
    )(offsets, directory, model_store)
    picked, own, traces = lax.optimization_barrier((picked, own, traces))
    coef_own = lax.all_to_all(picked, "shot", split_axis=0, concat_axis=0, tiled=True)
    own = pl.pallas_call(
        waves_kernel,
        out_shape=shape(10, own_rows, 128),
        in_specs=[VMEM],
        out_specs=VMEM,
        compiler_params=PARAMS,
    )(own)
    left, right = neighbours(own, "slab")
    inject = pl.pallas_call(
        inject_kernel,
        out_shape=shape(STEPS, 128),
        in_specs=[VMEM] * 3,
        out_specs=VMEM,
        compiler_params=LARGE,
    )(traces[0], rec_tile.reshape(1, -1), rec_col)
    coef_own, inject = lax.optimization_barrier((coef_own, inject + exchanged(inject, 1)))
    inject = inject + exchanged(inject, 2)
    inject_far = exchanged(inject, 4)
    slab = lax.axis_index("slab").astype(jnp.int32).reshape(1)
    coef_left, coef_right = neighbours(coef_own, "slab")
    coef = pl.pallas_call(
        functools.partial(coef_kernel, slabs),
        out_shape=shape(8, HELD * ROWS, 128),
        in_specs=[SMEM] + [VMEM] * 3,
        out_specs=VMEM,
        compiler_params=PARAMS,
        cost_estimate=pl.CostEstimate(flops=0, bytes_accessed=6 << 20, transcendentals=0),
    )(slab, coef_left, coef_own, coef_right)
    inject_far, coef = lax.optimization_barrier((inject_far, coef))
    inject = inject + inject_far
    state, image = pl.pallas_call(
        first_kernel,
        out_shape=(shape(10, own_rows, 128), shape(own_rows, 128)),
        in_specs=[SMEM, SMEM] + [ANY] * 3 + [VMEM],
        out_specs=(VMEM,) * 2,
        scratch_shapes=scratch(),
        compiler_params=PARAMS,
    )(slab, inject, left, own, right, coef)
    state_left, state_right = neighbours(state, "slab")
    state, pieces = pl.pallas_call(
        second_kernel,
        out_shape=(shape(10, own_rows, 128), shape(TILES, COLS, 128)),
        in_specs=[SMEM, SMEM] + [ANY] * 3 + [VMEM] * 2,
        out_specs=(VMEM,) * 2,
        scratch_shapes=scratch(),
        compiler_params=PARAMS,
    )(slab, inject, state_left, state, state_right, coef, image)
    pieces = lax.all_to_all(pieces, "shot", split_axis=0, concat_axis=0, tiled=True)
    waves_out = pl.pallas_call(
        final_kernel,
        out_shape=shape(10, COLS, depth),
        in_specs=[VMEM],
        out_specs=VMEM,
        compiler_params=PARAMS,
    )(state)
    stacked = pl.pallas_call(
        stack_kernel,
        out_shape=shape(model_store.shape[1], COLS, 128),
        in_specs=[SMEM, VMEM],
        out_specs=VMEM,
        compiler_params=PARAMS,
    )(offsets, pieces)
    return waves_out.reshape(waves.shape), stacked


def solution(mesh):
    placed = (
        P("shot", None, None, "slab", None),
        P("shot", None, "slab"),
        P("shot", "slab", None),
        P("shot", "slab"),
        P(),
        P(),
        P(None, None, "slab", "shot"),
    )
    return jax.shard_map(
        local,
        mesh=mesh,
        in_specs=placed,
        out_specs=(P("shot", None, None, "slab", None), P(None, "slab", "shot")),
        check_vma=False,
    )
```
